32 devices in a mesh: band: 8 (over z, y), det: 4 (over x, core).
Axes of the slice: x: 2, y: 2, z: 4, core: 2. Of those that a mesh axis runs over, the one named last changes fastest.
Arguments:
- sky_coeffs: float32 [3, 2, 8, 2048], P(None, None, 'band', 'det'), may hold values from -6 to 6
- beam_coeffs: bfloat16 [4, 3, 2, 17, 2048], P('det'), may hold values from -2.5 to 2.5
- wigner_panel: bfloat16 [8, 17, 2048, 8], P('band', None, 'det'), may hold values from -0.125 to 0.125
- m_values: int32 [8], replicated, may hold values from 0 to 4095, as said below
- cycle_table: int32 [8, 3], replicated, may hold values from -1 to 7, as said below
- send_lists: int32 [4, 8, 8, 2], P('det'), may hold values from -1 to 12287, as said below
- sample_block: int32 [4, 32768], P('det', 'band'), may hold values from 0 to 15, as said below
- sample_phi: int32 [4, 32768], P('det', 'band'), may hold values from 0 to 126
- sample_psi: int32 [4, 32768], P('det', 'band'), may hold values from 0 to 31
- sample_frac: float32 [2, 4, 32768], P(None, 'det', 'band'), may hold values from 0 to 1
Outputs:
- timestream: float32 [4, 32768], P('det', 'band')
The draws below stay inside these ranges and needn't reach their ends.
Inputs may be any that keep to these rules, and one draw needn't show every extreme that they name: `cycle_table`: each cycle stands in exactly one slot; -1 marks an empty slot; some cycle band fills all 3 slots, many hold none. `send_lists`: of one detector's entries from all bands to one owner, at most 8 are not -1, and every owner reaches 8; an entry from a band that holds no cycle is -1; an entry that is not -1 is slot * 4096 + start, with slot a filled slot of band src and start the block's first phi cell. `sample_block`: src * 2 + entry of an entry that is not -1 in the detector's list from band src to the sample's owner. `m_values`: distinct orders; 0 and 4095 among them.
All inputs are finite; a program needn't handle non-finite values.
Results may differ from the reference program's by a relative error of at most 0.0051.
Values may be sent and summed in bfloat16 or wider, within the bound.
No kernel may reach another device: no remote copies, remote signals or barrier semaphores. Data moves between devices by JAX's collectives and lax.ppermute only.
A program may use at most 64 MiB of HBM per device.

```python
import math
import jax
import jax.numpy as jnp
from jax import lax

COMP = 3
L = 2048
LMAX = 4096
BMAX = 8
MPRIME = 17
NPSI = 32
NPHI = 4096
M_ALL = 8
NDET = 4
CYCLES = 8
CYCLE_SLOTS = 3
LIST_LEN = 2
LISTED = 8
BLOCK_PHI = 128
S_DEV = 4096
NSAMP = 32768
N_BAND = 8


def cycle_layout(key):
    base = jax.random.fold_in(key, 7)
    first_key, second_key, third_key = jax.random.split(base, 3)
    middle = (jax.random.permutation(first_key, N_BAND - 2) + 1).astype(jnp.int32)
    full_band = middle[0]
    extra_band = middle[1]
    cycle_order = jax.random.permutation(second_key, CYCLES).astype(jnp.int32)
    total = N_BAND * CYCLE_SLOTS
    slot_ids = jnp.arange(total, dtype=jnp.int32)
    slot_band = slot_ids // CYCLE_SLOTS
    slot_place = slot_ids % CYCLE_SLOTS
    shuffled = jax.random.permutation(third_key, total).astype(jnp.int32)
    opener = (slot_place == 0) & ((slot_band == 0) | (slot_band == N_BAND - 1) | (slot_band == extra_band))
    priority = jnp.where((slot_band == full_band) | opener, shuffled - total, shuffled)
    chosen = jnp.argsort(priority)[:CYCLES]
    table = jnp.full((total,), -1, jnp.int32).at[chosen].set(cycle_order)
    return table.reshape(N_BAND, CYCLE_SLOTS)


def listing(key):
    table = cycle_layout(key)
    filled = table >= 0
    counts = jnp.sum(filled.astype(jnp.int32), 1)
    first_slot = jnp.argmax(filled.astype(jnp.int32), 1).astype(jnp.int32)
    slot_key, start_key, pick_key = jax.random.split(jax.random.fold_in(key, 19), 3)
    shape = (NDET, N_BAND, N_BAND, LIST_LEN)
    wanted = jax.random.randint(slot_key, shape, 0, CYCLE_SLOTS)
    sources = jnp.broadcast_to(jnp.arange(N_BAND, dtype=jnp.int32)[None, :, None, None], shape)
    slot_index = jnp.where(filled[sources, wanted], wanted, first_slot[sources])
    starts = jax.random.randint(start_key, shape, 0, NPHI)
    codes = (slot_index * NPHI + starts).astype(jnp.int32)
    entry_count = N_BAND * LIST_LEN
    valid = jnp.transpose(counts[sources] > 0, (0, 2, 1, 3)).reshape(NDET, N_BAND, entry_count)
    entry_ids = jnp.arange(entry_count, dtype=jnp.int32)
    scores = jax.random.randint(pick_key, (NDET, N_BAND, entry_count), 0, 2 ** 20) * entry_count + entry_ids[None, None, :]
    full = jnp.argmax(counts).astype(jnp.int32)
    scores = scores.at[0, 0, full * LIST_LEN].set(-3)
    scores = scores.at[0, 0, 0].set(-2)
    scores = scores.at[0, 0, entry_count - 1].set(-1)
    keyed = jnp.where(valid, scores, scores + 2 ** 29)
    order = jnp.argsort(keyed, axis=-1).astype(jnp.int32)
    rank = jnp.argsort(order, axis=-1).astype(jnp.int32)
    picked = rank < LISTED
    listed = jnp.transpose(picked.reshape(NDET, N_BAND, N_BAND, LIST_LEN), (0, 2, 1, 3))
    lists = jnp.where(listed, codes, -1).astype(jnp.int32)
    lists = lists.at[0, full, 0, 0].set(CYCLE_SLOTS * NPHI - 1)
    return (lists.astype(jnp.int32), order[:, :, :LISTED])


def draw_cycle_table(key, part):
    return cycle_layout(key)


def draw_m_values(key, part):
    inner = jax.random.permutation(jax.random.fold_in(key, 3), LMAX - 2)[:M_ALL - 2] + 1
    values = jnp.concatenate([jnp.array([0, LMAX - 1], dtype=jnp.int32), inner.astype(jnp.int32)])
    return jax.random.permutation(jax.random.fold_in(key, 5), values).astype(jnp.int32)


def draw_send_lists(key, part):
    lists, chosen = listing(key)
    return lists


def draw_sample_block(key, part):
    lists, chosen = listing(key)
    picks = jax.random.randint(jax.random.fold_in(key, 23), (NDET, NSAMP), 0, LISTED)
    owners = jnp.arange(NSAMP, dtype=jnp.int32) // S_DEV
    detectors = jnp.arange(NDET, dtype=jnp.int32)
    blocks = chosen[detectors[:, None], owners[None, :], picks]
    blocks = blocks.at[0, 0].set(0)
    blocks = blocks.at[0, 1].set(N_BAND * LIST_LEN - 1)
    return blocks.astype(jnp.int32)


def plant(entries, rng, smallest, top_value):
    longest = entries.shape.index(max(entries.shape))
    spots = []
    for shift in (0, 1):
        where = [jax.random.randint(jax.random.fold_in(rng, axis), (), 0, length) for axis, length in enumerate(entries.shape)]
        where[longest] = (where[longest] + shift) % entries.shape[longest]
        spots.append(tuple(where))
    return entries.at[spots[0]].set(smallest).at[spots[1]].set(top_value)


def shard_levels(stream_key, extent, cuts, least, high):
    gain = 1.0
    for dim, blocks in cuts:
        draws = jax.random.uniform(jax.random.fold_in(jax.random.fold_in(stream_key, 6), dim), (blocks,), jnp.float32, least / len(cuts), high / len(cuts))
        gain = gain * jnp.repeat(jnp.exp(draws), extent[dim] // blocks).reshape((-1,) + (1,) * (len(extent) - 1 - dim))
    return gain


def gaussian(key, shape, deviation, most, shards=(), kind=jnp.bfloat16):
    values = deviation * jax.random.normal(key, shape, jnp.float32)
    if shards:
        values = values * shard_levels(key, shape, shards, -0.22, 0.18)
    return jnp.clip(values, -most, most).astype(kind)


def setup_inputs(seed: int = 0) -> dict:
    arg_keys = jax.random.split(jax.random.key(seed), 11)
    return {
        "sky_coeffs": gaussian(arg_keys[0], (COMP, 2, M_ALL, L), 1.0, 6.0, ((2, 8), (3, 4)), jnp.float32),
        "beam_coeffs": gaussian(arg_keys[1], (NDET, COMP, 2, MPRIME, L), 0.4, 2.5, ((0, 4),)),
        "wigner_panel": gaussian(arg_keys[2], (M_ALL, MPRIME, L, CYCLES), L ** -0.5, 0.125, ((0, 8), (2, 4))),
        "m_values": draw_m_values(jax.random.fold_in(arg_keys[10], 71), 0),
        "cycle_table": draw_cycle_table(jax.random.fold_in(arg_keys[10], 71), 0),
        "send_lists": draw_send_lists(jax.random.fold_in(arg_keys[10], 71), 0),
        "sample_block": draw_sample_block(jax.random.fold_in(arg_keys[10], 71), 0),
        "sample_phi": plant(jax.random.randint(arg_keys[7], (NDET, NSAMP), 0, BLOCK_PHI - 1), jax.random.fold_in(arg_keys[7], 1), 0, (BLOCK_PHI - 1) - 1).astype(jnp.int32),
        "sample_psi": plant(jax.random.randint(arg_keys[8], (NDET, NSAMP), 0, NPSI), jax.random.fold_in(arg_keys[8], 1), 0, NPSI - 1).astype(jnp.int32),
        "sample_frac": jnp.clip(1.0 * jax.random.uniform(arg_keys[9], (2, NDET, NSAMP), jnp.float32) ** shard_levels(arg_keys[9], (2, NDET, NSAMP), ((1, 4), (2, 8)), -0.2, 0.2), 0.0, 1.0),
    }


def psi_apply(coef):
    highest = lax.Precision.HIGHEST
    cells = jnp.arange(NPSI, dtype=jnp.int32)
    orders = jnp.arange(MPRIME, dtype=jnp.int32) - BMAX
    turns = orders[:, None] * cells[None, :] % NPSI
    angle = 2.0 * math.pi / NPSI * turns.astype(jnp.float32)
    cos_psi = jnp.cos(angle)
    sin_psi = jnp.sin(angle)
    real_part = jnp.einsum('mnr,nj->mrj', coef[0], cos_psi, precision=highest) - jnp.einsum('mnr,nj->mrj', coef[1], sin_psi, precision=highest)
    imag_part = jnp.einsum('mnr,nj->mrj', coef[0], sin_psi, precision=highest) + jnp.einsum('mnr,nj->mrj', coef[1], cos_psi, precision=highest)
    return jnp.stack([real_part, imag_part], 0).astype(jnp.bfloat16)

def phi_table(m_values, columns):
    turns = m_values[:, None] * columns[None, :] % NPHI
    angle = 2.0 * math.pi / NPHI * turns.astype(jnp.float32)
    return jnp.concatenate([jnp.cos(angle), -jnp.sin(angle)], 0).astype(jnp.bfloat16)

def reference(sky_coeffs, beam_coeffs, wigner_panel, m_values, cycle_table, send_lists, sample_block, sample_phi, sample_psi, sample_frac):
    highest = lax.Precision.HIGHEST
    beams = beam_coeffs.astype(jnp.float32)
    mix_real = jnp.einsum('cmk,dcnk->dmnk', sky_coeffs[:, 0], beams[:, :, 0], precision=highest) + jnp.einsum('cmk,dcnk->dmnk', sky_coeffs[:, 1], beams[:, :, 1], precision=highest)
    mix_imag = jnp.einsum('cmk,dcnk->dmnk', sky_coeffs[:, 1], beams[:, :, 0], precision=highest) - jnp.einsum('cmk,dcnk->dmnk', sky_coeffs[:, 0], beams[:, :, 1], precision=highest)
    mixed = jnp.stack([mix_real, mix_imag], 1).astype(jnp.bfloat16)
    per_order = jnp.moveaxis(mixed, 2, 0)

    def one_order(pair):
        rows, panel = pair
        return jnp.einsum('dsnk,nkr->dsnr', rows.astype(jnp.float32), panel.astype(jnp.float32), precision=highest)
    coeff = lax.map(one_order, (per_order, wigner_panel))
    scale = 2.0 / math.sqrt(M_ALL * MPRIME)
    table = phi_table(m_values, jnp.arange(NPHI, dtype=jnp.int32)).astype(jnp.float32)
    owners = jnp.arange(NSAMP, dtype=jnp.int32) // S_DEV
    results = []
    for detector in range(NDET):
        upsi = psi_apply(jnp.transpose(coeff[:, detector], (1, 0, 2, 3)))
        rows = jnp.transpose(upsi, (2, 3, 0, 1)).reshape(CYCLES * NPSI, 2 * M_ALL).astype(jnp.float32)
        cube = (jnp.dot(rows, table, precision=highest) * scale).astype(jnp.bfloat16)
        flat_cube = cube.reshape(-1)
        lists = send_lists[detector]
        block = sample_block[detector]
        source = block // LIST_LEN
        entry = block % LIST_LEN
        code = lists[source, owners, entry]
        cycle = cycle_table[source, code // NPHI]
        phi_lo = (code % NPHI + sample_phi[detector]) % NPHI
        phi_hi = (phi_lo + 1) % NPHI
        psi_lo = sample_psi[detector]
        psi_hi = (psi_lo + 1) % NPSI
        low_base = (cycle * NPSI + psi_lo) * NPHI
        high_base = (cycle * NPSI + psi_hi) * NPHI
        value_ll = jnp.take(flat_cube, low_base + phi_lo).astype(jnp.float32)
        value_lh = jnp.take(flat_cube, low_base + phi_hi).astype(jnp.float32)
        value_hl = jnp.take(flat_cube, high_base + phi_lo).astype(jnp.float32)
        value_hh = jnp.take(flat_cube, high_base + phi_hi).astype(jnp.float32)
        frac_p = sample_frac[0, detector]
        frac_q = sample_frac[1, detector]
        low_row = (1.0 - frac_p) * value_ll + frac_p * value_lh
        high_row = (1.0 - frac_p) * value_hl + frac_p * value_hh
        results.append((1.0 - frac_q) * low_row + frac_q * high_row)
    return jnp.stack(results, 0)
```

```python
import math

import jax
import jax.numpy as jnp
from jax import lax
from jax.experimental import pallas as pl
from jax.experimental.pallas import tpu as pltpu
from jax.sharding import PartitionSpec as P

BMAX = 8
MPRIME = 17
NPSI = 32
NPHI = 4096
BLOCK_PHI = 128
LANES = 128
ROWS = 24


def psi_tables():
    cells = jnp.arange(NPSI, dtype=jnp.int32)
    orders = jnp.arange(MPRIME, dtype=jnp.int32) - BMAX
    turns = orders[:, None] * cells[None, :] % NPSI
    angle = 2.0 * math.pi / NPSI * turns.astype(jnp.float32)
    return (jnp.cos(angle), jnp.sin(angle))


def psi_items(incoming):
    highest = lax.Precision.HIGHEST
    cos_psi, sin_psi = psi_tables()
    real_part = jnp.einsum(
        "bimn,nj->bimj", incoming[:, :, 0], cos_psi, precision=highest
    ) - jnp.einsum("bimn,nj->bimj", incoming[:, :, 1], sin_psi, precision=highest)
    imag_part = jnp.einsum(
        "bimn,nj->bimj", incoming[:, :, 0], sin_psi, precision=highest
    ) + jnp.einsum("bimn,nj->bimj", incoming[:, :, 1], cos_psi, precision=highest)
    return jnp.stack([real_part, imag_part], 2).astype(jnp.bfloat16)


def phi_table(m_values, columns):
    turns = m_values[:, None] * columns[None, :] % NPHI
    angle = 2.0 * math.pi / NPHI * turns.astype(jnp.float32)
    return jnp.concatenate([jnp.cos(angle), -jnp.sin(angle)], 0).astype(jnp.bfloat16)


def cycle_cube(samples, table, scale):
    bands, items, parts, local_orders, cells = samples.shape
    rows = jnp.transpose(samples, (1, 4, 2, 0, 3)).reshape(
        items * cells, parts * bands * local_orders
    )
    values = jnp.dot(rows, table, preferred_element_type=jnp.float32) * scale
    return values.astype(jnp.bfloat16).reshape(items, cells, table.shape[1])


def interpolate(flat_cells, block_pos, cell_phi, cell_psi, frac_phi, frac_psi):
    psi_next = (cell_psi + 1) % NPSI
    base_index = block_pos * (NPSI * BLOCK_PHI)
    low_index = base_index + cell_psi * BLOCK_PHI + cell_phi
    high_index = base_index + psi_next * BLOCK_PHI + cell_phi
    value_ll = jnp.take(flat_cells, low_index).astype(jnp.float32)
    value_lh = jnp.take(flat_cells, low_index + 1).astype(jnp.float32)
    value_hl = jnp.take(flat_cells, high_index).astype(jnp.float32)
    value_hh = jnp.take(flat_cells, high_index + 1).astype(jnp.float32)
    low_row = (1.0 - frac_phi) * value_ll + frac_phi * value_lh
    high_row = (1.0 - frac_phi) * value_hl + frac_phi * value_hh
    return (1.0 - frac_psi) * low_row + frac_psi * high_row


def by_blocks(
    sky_coeffs,
    beam_coeffs,
    wigner_panel,
    m_values,
    cycle_table,
    send_lists,
    sample_block,
    sample_phi,
    sample_psi,
    sample_frac,
):
    highest = lax.Precision.HIGHEST
    orders_all = m_values.shape[0]
    scale = 2.0 / math.sqrt(orders_all * MPRIME)
    own_band = lax.axis_index("band")
    beams = lax.all_to_all(beam_coeffs, "det", split_axis=4, concat_axis=0, tiled=True).astype(
        jnp.float32
    )
    mix_real = jnp.einsum(
        "cmk,dcnk->dmnk", sky_coeffs[:, 0], beams[:, :, 0], precision=highest
    ) + jnp.einsum("cmk,dcnk->dmnk", sky_coeffs[:, 1], beams[:, :, 1], precision=highest)
    mix_imag = jnp.einsum(
        "cmk,dcnk->dmnk", sky_coeffs[:, 1], beams[:, :, 0], precision=highest
    ) - jnp.einsum("cmk,dcnk->dmnk", sky_coeffs[:, 0], beams[:, :, 1], precision=highest)
    mixed = jnp.stack([mix_real, mix_imag], 1).astype(jnp.bfloat16)
    coeff = lax.psum_scatter(
        jnp.einsum("dsmnk,mnkr->dsmnr", mixed, wigner_panel, preferred_element_type=jnp.float32),
        "det",
        scatter_dimension=0,
        tiled=True,
    )[0]
    lists = send_lists[0]
    cycle_index = jnp.maximum(cycle_table, 0)
    table = phi_table(m_values, jnp.arange(NPHI, dtype=jnp.int32))
    payload = jnp.transpose(jnp.take(coeff, cycle_index, axis=3), (3, 4, 0, 1, 2))
    cube = cycle_cube(
        psi_items(lax.all_to_all(payload, "band", split_axis=0, concat_axis=0, tiled=True)),
        table,
        scale,
    )
    my_codes = jnp.maximum(lax.dynamic_index_in_dim(lists, own_band, 0, keepdims=False), 0)
    slot_index = my_codes // NPHI
    start_cell = my_codes % NPHI
    wrapped = jnp.concatenate([cube, cube[:, :, :BLOCK_PHI]], 2)

    def cut_block(slot_one, start_one):
        return lax.dynamic_slice(wrapped, (slot_one, 0, start_one), (1, NPSI, BLOCK_PHI))[0]

    outgoing = jax.vmap(jax.vmap(cut_block))(slot_index, start_cell)
    received = lax.all_to_all(outgoing, "band", split_axis=0, concat_axis=0, tiled=True)
    flat_cells = received.reshape(-1)
    block_pos = sample_block[0]
    values = interpolate(
        flat_cells, block_pos, sample_phi[0], sample_psi[0], sample_frac[0, 0], sample_frac[1, 0]
    )
    return values[None, :]


def smem():
    return pl.BlockSpec(memory_space=pltpu.SMEM)


def vmem():
    return pl.BlockSpec(memory_space=pltpu.VMEM)


def cos_sin(turns, whole):
    quarter = whole // 4
    quadrant = (turns + quarter // 2) // quarter
    rest = turns - quadrant * quarter
    x = rest.astype(jnp.float32) * (2.0 * math.pi / whole)
    y = x * x
    sine = x * (1.0 + y * (-1.0 / 6 + y * (1.0 / 120 + y * (-1.0 / 5040 + y * (1.0 / 362880)))))
    cosine = 1.0 + y * (
        -0.5 + y * (1.0 / 24 + y * (-1.0 / 720 + y * (1.0 / 40320 - y * (1.0 / 3628800))))
    )
    quadrant = quadrant & 3
    odd = (quadrant & 1) == 1
    c = jnp.where(odd, sine, cosine)
    s = jnp.where(odd, cosine, sine)
    c = jnp.where((quadrant == 1) | (quadrant == 2), -c, c)
    s = jnp.where(quadrant >= 2, -s, s)
    return c, s


def beam_kernel(place, own, other, out):
    chunk = out.shape[4] // 2
    for side, ref in enumerate((own, other)):
        for part in range(2):
            owner = place[0] ^ (2 * part)
            lanes = pl.ds(pl.multiple_of(owner * chunk, chunk), chunk)
            for c in range(ref.shape[0]):
                block = ref[c, :, :, lanes].astype(jnp.float32)
                for s in range(2):
                    out[side, c, s, 0:MPRIME, part * chunk : (part + 1) * chunk] = block[:, s, :]
    out[:, :, :, MPRIME:, :] = jnp.zeros_like(out[:, :, :, MPRIME:, :])


def sample_kernel(
    place, m_values, cycle_table, lists, block, phi, psi, frac, phase, low, high, tables
):
    orders = m_values.shape[0]
    slots = cycle_table.shape[0] // orders
    scale = 2.0 / math.sqrt(orders * MPRIME)
    band = place[1]
    blocks = block[...]
    start = jnp.zeros_like(blocks)
    cycle = jnp.zeros_like(blocks)
    entries = lists.shape[0] // (orders * orders)
    for source in range(orders):
        for entry in range(entries):
            code = jnp.maximum(lists[(source * orders + band) * entries + entry], 0)
            here = blocks == source * entries + entry
            start = jnp.where(here, code & (NPHI - 1), start)
            cycle = jnp.where(here, cycle_table[source * slots + lax.div(code, NPHI)], cycle)
    cell = psi[...]
    low[...] = cycle * NPSI + cell
    high[...] = cycle * NPSI + ((cell + 1) & (NPSI - 1))
    first = (start + phi[...]) & (NPHI - 1)
    row = lax.broadcasted_iota(jnp.int32, (orders, LANES), 0)
    m = jnp.zeros((orders, LANES), jnp.int32)
    for k in range(orders):
        m = jnp.where(row == k, m_values[band ^ k], m)
    for g in range(blocks.shape[0]):
        turns = (m * first[g : g + 1, :]) & (NPHI - 1)
        c0, s0 = cos_sin(turns, NPHI)
        c1, s1 = cos_sin((turns + m) & (NPHI - 1), NPHI)
        c0, s0, c1, s1 = (v.astype(jnp.bfloat16).astype(jnp.float32) for v in (c0, s0, c1, s1))
        f = frac[0, g : g + 1, :]
        e = 1.0 - f
        phase[g, 0] = (e * c0 + f * c1) * scale
        phase[g, 1] = (e * s0 + f * s1) * (-scale)
    shape = tables.shape[1:]
    lane = lax.broadcasted_iota(jnp.int32, shape, 1) & (NPSI - 1)
    line = lax.broadcasted_iota(jnp.int32, shape, 0)
    imag = line >= ROWS
    n = jnp.where(imag, line - ROWS, line)
    c, s = cos_sin(((n - BMAX) * lane) & (NPSI - 1), NPSI)
    tables[0] = jnp.where(imag, -s, c)
    tables[1] = jnp.where(imag, c, s)


def rows_kernel(beams, sky_own, sky_other, w_own, w_other, tables, mine, theirs):
    chunk = w_own.shape[1]
    cycles = w_own.shape[0] // MPRIME
    total = None
    for part, (sky, w) in enumerate(((sky_own, w_own), (sky_other, w_other))):
        lanes = slice(part * chunk, (part + 1) * chunk)
        pieces = []
        for side in range(2):
            real = jnp.zeros((ROWS, chunk), jnp.float32)
            imag = jnp.zeros((ROWS, chunk), jnp.float32)
            for c in range(sky.shape[0]):
                sr, si = sky[c, 0], sky[c, 1]
                br, bi = beams[side, c, 0, :, lanes], beams[side, c, 1, :, lanes]
                real += sr * br + si * bi
                imag += si * br - sr * bi
            pieces += [real, imag]
        mixed = jnp.concatenate(pieces, 0).astype(jnp.bfloat16)
        term = lax.dot_general(
            mixed, w[...], (((1,), (1,)), ((), ())), preferred_element_type=jnp.float32
        )
        total = term if total is None else total + term
    line = lax.broadcasted_iota(jnp.int32, total.shape, 0)
    column = lax.broadcasted_iota(jnp.int32, total.shape, 1)
    kept = jnp.where(lax.rem(line, ROWS) == lax.div(column, cycles), total, 0.0)
    wide = (w_own.shape[0], cycles * NPSI)
    spread = (
        lax.rem(lax.broadcasted_iota(jnp.int32, wide, 0), cycles)
        == lax.div(lax.broadcasted_iota(jnp.int32, wide, 1), NPSI)
    ).astype(jnp.bfloat16)
    coeff = jnp.zeros((total.shape[0], wide[1]), jnp.float32)
    for _ in range(3):
        piece = kept.astype(jnp.bfloat16)
        kept = kept - piece.astype(jnp.float32)
        coeff += jnp.dot(piece, spread, preferred_element_type=jnp.float32)
    for side, out in enumerate((mine, theirs)):
        own = coeff[side * 2 * ROWS : (side + 1) * 2 * ROWS]
        for s in range(2):
            out[s : s + 1, :] = jnp.sum(own * tables[s], 0, keepdims=True)


def final_kernel(*refs):
    *parts, phase, low, high, frac, out = refs
    width = parts[0].shape[2]
    rows = [part[k, :, :].astype(jnp.float32) for part in parts for k in range(part.shape[0])]
    planes = [jnp.concatenate([row[s : s + 1] for row in rows], 0) for s in range(2)]
    tiles = [[plane[:, t : t + LANES] for t in range(0, width, LANES)] for plane in planes]

    def pick(table, index):
        value = None
        inside = index & (LANES - 1)
        for t, tile in enumerate(table):
            found = jnp.take_along_axis(tile, inside, axis=1, mode="promise_in_bounds")
            value = found if value is None else jnp.where(index >= t * LANES, found, value)
        return value

    for g in range(out.shape[0]):
        shape = (len(rows), LANES)
        at_low = jnp.broadcast_to(low[g : g + 1, :], shape)
        at_high = jnp.broadcast_to(high[g : g + 1, :], shape)
        f = frac[1, g : g + 1, :]
        e = 1.0 - f
        real = e * pick(tiles[0], at_low) + f * pick(tiles[0], at_high)
        imag = e * pick(tiles[1], at_low) + f * pick(tiles[1], at_high)
        total = real * phase[g, 0] + imag * phase[g, 1]
        out[g : g + 1, :] = jnp.sum(total, 0, keepdims=True)


def call(kernel, out_shape, in_specs, flops):
    return pl.pallas_call(
        kernel,
        out_shape=out_shape,
        in_specs=in_specs,
        out_specs=jax.tree.map(lambda _: vmem(), out_shape),
        cost_estimate=pl.CostEstimate(flops=flops, bytes_accessed=1 << 20, transcendentals=0),
        compiler_params=pltpu.CompilerParams(vmem_limit_bytes=24 << 20),
    )


def by_samples(
    sky_coeffs,
    beam_coeffs,
    wigner_panel,
    m_values,
    cycle_table,
    send_lists,
    sample_block,
    sample_phi,
    sample_psi,
    sample_frac,
):
    f32 = jnp.float32
    bands = lax.axis_size("band")
    band, det = lax.axis_index("band"), lax.axis_index("det")
    place = jnp.stack([det, band])
    chunk, cycles = wigner_panel.shape[2:]
    groups = sample_block.shape[1] // LANES
    psi_width = cycles * NPSI

    def swap(x, axis, bit):
        return lax.ppermute(x, axis, [(i, i ^ bit) for i in range(lax.axis_size(axis))])

    panel = jnp.transpose(wigner_panel[0], (0, 2, 1)).reshape(MPRIME * cycles, chunk)
    beam = jnp.transpose(beam_coeffs[0], (0, 2, 1, 3))
    panel_other = swap(panel, "det", 2)
    sky_other = swap(sky_coeffs, "det", 2)
    beam_other = swap(beam, "det", 1)

    phase, low, high, tables = call(
        sample_kernel,
        (
            jax.ShapeDtypeStruct((groups, 2, bands, LANES), f32),
            jax.ShapeDtypeStruct((groups, LANES), jnp.int32),
            jax.ShapeDtypeStruct((groups, LANES), jnp.int32),
            jax.ShapeDtypeStruct((2, 2 * ROWS, psi_width), f32),
        ),
        [smem()] * 4 + [vmem()] * 4,
        1 << 22,
    )(
        place,
        m_values,
        cycle_table.reshape(-1),
        send_lists.reshape(-1),
        sample_block.reshape(groups, LANES),
        sample_phi.reshape(groups, LANES),
        sample_psi.reshape(groups, LANES),
        sample_frac.reshape(2, groups, LANES),
    )
    beams = call(
        beam_kernel,
        jax.ShapeDtypeStruct((2, beam.shape[0], 2, ROWS, 2 * chunk), f32),
        [smem(), vmem(), vmem()],
        1 << 22,
    )(place, beam, beam_other)
    mine, theirs = call(
        rows_kernel,
        (jax.ShapeDtypeStruct((2, psi_width), f32), jax.ShapeDtypeStruct((2, psi_width), f32)),
        [vmem()] * 6,
        1 << 22,
    )(beams, sky_coeffs, sky_other, panel, panel_other, tables)
    rows = (mine + swap(theirs, "det", 1)).astype(jnp.bfloat16)
    pair = jnp.stack([rows, swap(rows, "band", 1)])
    parts = [pair] + [swap(pair, "band", k) for k in range(2, bands, 2)]
    values = call(
        final_kernel,
        jax.ShapeDtypeStruct((groups, LANES), f32),
        [vmem()] * (len(parts) + 4),
        1 << 22,
    )(*parts, phase, low, high, sample_frac.reshape(2, groups, LANES))
    return values.reshape(1, -1)


def solution(mesh):
    def per_device(*args):
        cycles = args[2].shape[3]
        small = mesh.shape["band"] <= 8 and cycles <= 8
        return (by_samples if small else by_blocks)(*args)

    return jax.shard_map(
        per_device,
        mesh=mesh,
        in_specs=(
            P(None, None, "band", "det"),
            P("det", None, None, None, None),
            P("band", None, "det", None),
            P(),
            P(),
            P("det", None, None, None),
            P("det", "band"),
            P("det", "band"),
            P("det", "band"),
            P(None, "det", "band"),
        ),
        out_specs=P("det", "band"),
        check_vma=False,
    )
```

```python
import math

import jax
import jax.numpy as jnp
from jax import lax
from jax.experimental import pallas as pl
from jax.experimental.pallas import tpu as pltpu
from jax.sharding import PartitionSpec as P

BMAX = 8
MPRIME = 17
NPSI = 32
NPHI = 4096
BLOCK_PHI = 128
LANES = 128
ROWS = 24


def psi_tables():
    cells = jnp.arange(NPSI, dtype=jnp.int32)
    orders = jnp.arange(MPRIME, dtype=jnp.int32) - BMAX
    turns = orders[:, None] * cells[None, :] % NPSI
    angle = 2.0 * math.pi / NPSI * turns.astype(jnp.float32)
    return (jnp.cos(angle), jnp.sin(angle))


def psi_items(incoming):
    highest = lax.Precision.HIGHEST
    cos_psi, sin_psi = psi_tables()
    real_part = jnp.einsum(
        "bimn,nj->bimj", incoming[:, :, 0], cos_psi, precision=highest
    ) - jnp.einsum("bimn,nj->bimj", incoming[:, :, 1], sin_psi, precision=highest)
    imag_part = jnp.einsum(
        "bimn,nj->bimj", incoming[:, :, 0], sin_psi, precision=highest
    ) + jnp.einsum("bimn,nj->bimj", incoming[:, :, 1], cos_psi, precision=highest)
    return jnp.stack([real_part, imag_part], 2).astype(jnp.bfloat16)


def phi_table(m_values, columns):
    turns = m_values[:, None] * columns[None, :] % NPHI
    angle = 2.0 * math.pi / NPHI * turns.astype(jnp.float32)
    return jnp.concatenate([jnp.cos(angle), -jnp.sin(angle)], 0).astype(jnp.bfloat16)


def cycle_cube(samples, table, scale):
    bands, items, parts, local_orders, cells = samples.shape
    rows = jnp.transpose(samples, (1, 4, 2, 0, 3)).reshape(
        items * cells, parts * bands * local_orders
    )
    values = jnp.dot(rows, table, preferred_element_type=jnp.float32) * scale
    return values.astype(jnp.bfloat16).reshape(items, cells, table.shape[1])


def interpolate(flat_cells, block_pos, cell_phi, cell_psi, frac_phi, frac_psi):
    psi_next = (cell_psi + 1) % NPSI
    base_index = block_pos * (NPSI * BLOCK_PHI)
    low_index = base_index + cell_psi * BLOCK_PHI + cell_phi
    high_index = base_index + psi_next * BLOCK_PHI + cell_phi
    value_ll = jnp.take(flat_cells, low_index).astype(jnp.float32)
    value_lh = jnp.take(flat_cells, low_index + 1).astype(jnp.float32)
    value_hl = jnp.take(flat_cells, high_index).astype(jnp.float32)
    value_hh = jnp.take(flat_cells, high_index + 1).astype(jnp.float32)
    low_row = (1.0 - frac_phi) * value_ll + frac_phi * value_lh
    high_row = (1.0 - frac_phi) * value_hl + frac_phi * value_hh
    return (1.0 - frac_psi) * low_row + frac_psi * high_row


def by_blocks(
    sky_coeffs,
    beam_coeffs,
    wigner_panel,
    m_values,
    cycle_table,
    send_lists,
    sample_block,
    sample_phi,
    sample_psi,
    sample_frac,
):
    highest = lax.Precision.HIGHEST
    orders_all = m_values.shape[0]
    scale = 2.0 / math.sqrt(orders_all * MPRIME)
    own_band = lax.axis_index("band")
    beams = lax.all_to_all(beam_coeffs, "det", split_axis=4, concat_axis=0, tiled=True).astype(
        jnp.float32
    )
    mix_real = jnp.einsum(
        "cmk,dcnk->dmnk", sky_coeffs[:, 0], beams[:, :, 0], precision=highest
    ) + jnp.einsum("cmk,dcnk->dmnk", sky_coeffs[:, 1], beams[:, :, 1], precision=highest)
    mix_imag = jnp.einsum(
        "cmk,dcnk->dmnk", sky_coeffs[:, 1], beams[:, :, 0], precision=highest
    ) - jnp.einsum("cmk,dcnk->dmnk", sky_coeffs[:, 0], beams[:, :, 1], precision=highest)
    mixed = jnp.stack([mix_real, mix_imag], 1).astype(jnp.bfloat16)
    coeff = lax.psum_scatter(
        jnp.einsum("dsmnk,mnkr->dsmnr", mixed, wigner_panel, preferred_element_type=jnp.float32),
        "det",
        scatter_dimension=0,
        tiled=True,
    )[0]
    lists = send_lists[0]
    cycle_index = jnp.maximum(cycle_table, 0)
    table = phi_table(m_values, jnp.arange(NPHI, dtype=jnp.int32))
    payload = jnp.transpose(jnp.take(coeff, cycle_index, axis=3), (3, 4, 0, 1, 2))
    cube = cycle_cube(
        psi_items(lax.all_to_all(payload, "band", split_axis=0, concat_axis=0, tiled=True)),
        table,
        scale,
    )
    my_codes = jnp.maximum(lax.dynamic_index_in_dim(lists, own_band, 0, keepdims=False), 0)
    slot_index = my_codes // NPHI
    start_cell = my_codes % NPHI
    wrapped = jnp.concatenate([cube, cube[:, :, :BLOCK_PHI]], 2)

    def cut_block(slot_one, start_one):
        return lax.dynamic_slice(wrapped, (slot_one, 0, start_one), (1, NPSI, BLOCK_PHI))[0]

    outgoing = jax.vmap(jax.vmap(cut_block))(slot_index, start_cell)
    received = lax.all_to_all(outgoing, "band", split_axis=0, concat_axis=0, tiled=True)
    flat_cells = received.reshape(-1)
    block_pos = sample_block[0]
    values = interpolate(
        flat_cells, block_pos, sample_phi[0], sample_psi[0], sample_frac[0, 0], sample_frac[1, 0]
    )
    return values[None, :]


def smem():
    return pl.BlockSpec(memory_space=pltpu.SMEM)


def hbm():
    return pl.BlockSpec(memory_space=pltpu.HBM)


def vmem():
    return pl.BlockSpec(memory_space=pltpu.VMEM)


def cos_sin(turns, whole):
    quarter = whole // 4
    quadrant = (turns + quarter // 2) // quarter
    rest = turns - quadrant * quarter
    x = rest.astype(jnp.float32) * (2.0 * math.pi / whole)
    y = x * x
    sine = x * (1.0 + y * (-1.0 / 6 + y * (1.0 / 120 + y * (-1.0 / 5040 + y * (1.0 / 362880)))))
    cosine = 1.0 + y * (
        -0.5 + y * (1.0 / 24 + y * (-1.0 / 720 + y * (1.0 / 40320 - y * (1.0 / 3628800))))
    )
    quadrant = quadrant & 3
    odd = (quadrant & 1) == 1
    c = jnp.where(odd, sine, cosine)
    s = jnp.where(odd, cosine, sine)
    c = jnp.where((quadrant == 1) | (quadrant == 2), -c, c)
    s = jnp.where(quadrant >= 2, -s, s)
    return c, s


def beam_kernel(place, source, out):
    chunk = out.shape[3] // 2
    for part in range(2):
        owner = place[0] ^ (2 * part)
        lanes = pl.ds(pl.multiple_of(owner * chunk, chunk), chunk)
        for c in range(out.shape[0]):
            block = source[c, :, :, lanes].astype(jnp.float32)
            for s in range(2):
                out[c, s, 0:MPRIME, part * chunk : (part + 1) * chunk] = block[:, s, :]
    out[:, :, MPRIME:, :] = jnp.zeros_like(out[:, :, MPRIME:, :])


def beam_copy_kernel(place, source, out, held, sem):
    copy = pltpu.make_async_copy(source, held, sem)
    copy.start()
    copy.wait()
    beam_kernel(place, held, out)


def sample_kernel(
    place, m_values, cycle_table, lists, *refs
):
    sources, (phase, low, high), (block, phi, psi, frac, sems) = refs[:4], refs[4:7], refs[7:]
    copies = [
        pltpu.make_async_copy(source, held, sems.at[i])
        for i, (source, held) in enumerate(zip(sources, (block, phi, psi, frac)))
    ]
    for copy in copies:
        copy.start()
    orders = m_values.shape[0]
    row = lax.broadcasted_iota(jnp.int32, (orders, LANES), 0)
    m = jnp.zeros((orders, LANES), jnp.int32)
    for k in range(orders):
        m = jnp.where(row == k, m_values[place[1] ^ k], m)
    for copy in copies:
        copy.wait()
    scale = 2.0 / math.sqrt(orders * MPRIME)
    band = place[1]
    blocks = block[...]
    start = jnp.zeros_like(blocks)
    cycle = jnp.zeros_like(blocks)
    sources, entries = lists.shape[:2]
    for source in range(sources):
        for entry in range(entries):
            code = jnp.maximum(lists[source, entry, band], 0)
            here = blocks == source * entries + entry
            start = jnp.where(here, code & (NPHI - 1), start)
            cycle = jnp.where(here, cycle_table[lax.div(code, NPHI), source], cycle)
    cell = psi[...]
    low[...] = cycle * NPSI + cell
    high[...] = cycle * NPSI + ((cell + 1) & (NPSI - 1))
    first = (start + phi[...]) & (NPHI - 1)
    for g in range(blocks.shape[0]):
        turns = (m * first[g : g + 1, :]) & (NPHI - 1)
        c0, s0 = cos_sin(turns, NPHI)
        c1, s1 = cos_sin((turns + m) & (NPHI - 1), NPHI)
        c0, s0, c1, s1 = (v.astype(jnp.bfloat16).astype(jnp.float32) for v in (c0, s0, c1, s1))
        f = frac[0, g : g + 1, :]
        e = 1.0 - f
        phase[g, 0] = (e * c0 + f * c1) * scale
        phase[g, 1] = (e * s0 + f * s1) * (-scale)


def psi_weights(width):
    shape = (2 * ROWS, width)
    lane = lax.broadcasted_iota(jnp.int32, shape, 1) & (NPSI - 1)
    line = lax.broadcasted_iota(jnp.int32, shape, 0)
    imag = line >= ROWS
    n = jnp.where(imag, line - ROWS, line)
    c, s = cos_sin(((n - BMAX) * lane) & (NPSI - 1), NPSI)
    return jnp.where(imag, -s, c), jnp.where(imag, c, s)


def rows_kernel(beam_own, beam_other, sky_own, sky_other, w_own, w_other, out):
    chunk = w_own.shape[1]
    cycles = w_own.shape[0] // MPRIME
    total = None
    for part, (sky, w) in enumerate(((sky_own, w_own), (sky_other, w_other))):
        lanes = slice(part * chunk, (part + 1) * chunk)
        pieces = []
        for beam in (beam_own, beam_other):
            real = jnp.zeros((ROWS, chunk), jnp.float32)
            imag = jnp.zeros((ROWS, chunk), jnp.float32)
            for c in range(sky.shape[0]):
                sr, si = sky[c, 0], sky[c, 1]
                br, bi = beam[c, 0, :, lanes], beam[c, 1, :, lanes]
                real += sr * br + si * bi
                imag += si * br - sr * bi
            pieces += [real, imag]
        mixed = jnp.concatenate(pieces, 0).astype(jnp.bfloat16)
        term = lax.dot_general(
            mixed, w[...], (((1,), (1,)), ((), ())), preferred_element_type=jnp.float32
        )
        total = term if total is None else total + term
    line = lax.broadcasted_iota(jnp.int32, total.shape, 0)
    column = lax.broadcasted_iota(jnp.int32, total.shape, 1)
    kept = jnp.where(lax.rem(line, ROWS) == lax.div(column, cycles), total, 0.0)
    wide = (w_own.shape[0], cycles * NPSI)
    spread = (
        lax.rem(lax.broadcasted_iota(jnp.int32, wide, 0), cycles)
        == lax.div(lax.broadcasted_iota(jnp.int32, wide, 1), NPSI)
    ).astype(jnp.bfloat16)
    coeff = jnp.zeros((total.shape[0], wide[1]), jnp.float32)
    for _ in range(3):
        piece = kept.astype(jnp.bfloat16)
        kept = kept - piece.astype(jnp.float32)
        coeff += jnp.dot(piece, spread, preferred_element_type=jnp.float32)
    weights = psi_weights(wide[1])
    for side in range(2):
        held = coeff[side * 2 * ROWS : (side + 1) * 2 * ROWS]
        for s in range(2):
            out[side, s : s + 1, :] = jnp.sum(held * weights[s], 0, keepdims=True)


def final_kernel(*refs):
    *parts, phase, low, high, frac, out = refs
    width = parts[0].shape[2]
    rows = [part[k, :, :].astype(jnp.float32) for part in parts for k in range(part.shape[0])]
    planes = [jnp.concatenate([row[s : s + 1] for row in rows], 0) for s in range(2)]
    tiles = [[plane[:, t : t + LANES] for t in range(0, width, LANES)] for plane in planes]

    def pick(table, index):
        value = None
        inside = index & (LANES - 1)
        for t, tile in enumerate(table):
            found = jnp.take_along_axis(tile, inside, axis=1, mode="promise_in_bounds")
            value = found if value is None else jnp.where(index >= t * LANES, found, value)
        return value

    for g in range(out.shape[0]):
        shape = (len(rows), LANES)
        at_low = jnp.broadcast_to(low[g : g + 1, :], shape)
        at_high = jnp.broadcast_to(high[g : g + 1, :], shape)
        f = frac[1, g : g + 1, :]
        e = 1.0 - f
        real = e * pick(tiles[0], at_low) + f * pick(tiles[0], at_high)
        imag = e * pick(tiles[1], at_low) + f * pick(tiles[1], at_high)
        total = real * phase[g, 0] + imag * phase[g, 1]
        out[g : g + 1, :] = jnp.sum(total, 0, keepdims=True)


def call(kernel, out_shape, in_specs, flops, scratch=()):
    return pl.pallas_call(
        kernel,
        out_shape=out_shape,
        in_specs=in_specs,
        out_specs=jax.tree.map(lambda _: vmem(), out_shape),
        scratch_shapes=scratch,
        cost_estimate=pl.CostEstimate(flops=flops, bytes_accessed=1 << 20, transcendentals=0),
        compiler_params=pltpu.CompilerParams(vmem_limit_bytes=24 << 20),
    )


def by_samples(
    sky_coeffs,
    beam_coeffs,
    wigner_panel,
    m_values,
    cycle_table,
    send_lists,
    sample_block,
    sample_phi,
    sample_psi,
    sample_frac,
):
    f32 = jnp.float32
    bands = lax.axis_size("band")
    band, det = lax.axis_index("band"), lax.axis_index("det")
    place = jnp.stack([det, band])
    chunk, cycles = wigner_panel.shape[2:]
    groups = sample_block.shape[1] // LANES
    psi_width = cycles * NPSI

    sizes = (bands, lax.axis_size("det"))

    def swap(x, band_bits, det_bits):
        pairs = [
            (b * sizes[1] + d, (b ^ band_bits) * sizes[1] + (d ^ det_bits))
            for b in range(sizes[0])
            for d in range(sizes[1])
        ]
        return lax.ppermute(x, ("band", "det"), pairs)

    panel = jnp.transpose(wigner_panel[0], (0, 2, 1)).reshape(MPRIME * cycles, chunk)
    beam = jnp.transpose(beam_coeffs[0], (0, 2, 1, 3))
    panel_other = swap(panel, 0, 2)
    sky_other = swap(sky_coeffs, 0, 2)
    beam, place = lax.optimization_barrier((beam, place))
    beam_other = swap(beam, 0, 1)
    split = jax.ShapeDtypeStruct((beam.shape[0], 2, ROWS, 2 * chunk), f32)
    beam_own = call(
        beam_copy_kernel,
        split,
        [smem(), hbm()],
        1 << 22,
        [pltpu.VMEM(beam.shape, beam.dtype), pltpu.SemaphoreType.DMA],
    )(place, beam)
    beam_other = call(beam_kernel, split, [smem(), vmem()], 1 << 22)(place, beam_other)
    sums = call(rows_kernel, jax.ShapeDtypeStruct((2, 2, psi_width), f32), [vmem()] * 6, 1 << 22)(
        beam_own, beam_other, sky_coeffs, sky_other, panel, panel_other
    )
    rows = (sums + swap(sums, 0, 1)[::-1]).astype(jnp.bfloat16)
    rows_y = swap(rows, 1, 1)
    block, phi, psi, frac, _ = lax.optimization_barrier(
        (sample_block, sample_phi, sample_psi, sample_frac, rows)
    )
    held = [pltpu.VMEM((groups, LANES), jnp.int32)] * 3 + [pltpu.VMEM((2, groups, LANES), f32)]
    phase, low, high = call(
        sample_kernel,
        (
            jax.ShapeDtypeStruct((groups, 2, bands, LANES), f32),
            jax.ShapeDtypeStruct((groups, LANES), jnp.int32),
            jax.ShapeDtypeStruct((groups, LANES), jnp.int32),
        ),
        [smem()] * 4 + [hbm()] * 4,
        1 << 22,
        held + [pltpu.SemaphoreType.DMA((4,))],
    )(
        place,
        m_values,
        cycle_table.T,
        jnp.transpose(send_lists[0], (0, 2, 1)),
        block.reshape(groups, LANES),
        phi.reshape(groups, LANES),
        psi.reshape(groups, LANES),
        frac.reshape(2, groups, LANES),
    )
    pair = jnp.stack([rows[0], rows_y[1]])
    pair_other = jnp.stack([rows[1], rows_y[0]])
    parts = [pair] + [swap(pair_other, k, 1) for k in range(2, bands, 2)]
    values = call(
        final_kernel,
        jax.ShapeDtypeStruct((groups, LANES), f32),
        [vmem()] * (len(parts) + 4),
        1 << 22,
    )(*parts, phase, low, high, sample_frac.reshape(2, groups, LANES))
    return values.reshape(1, -1)


def solution(mesh):
    def per_device(*args):
        cycles = args[2].shape[3]
        small = mesh.shape["band"] <= 8 and cycles <= 8
        return (by_samples if small else by_blocks)(*args)

    return jax.shard_map(
        per_device,
        mesh=mesh,
        in_specs=(
            P(None, None, "band", "det"),
            P("det", None, None, None, None),
            P("band", None, "det", None),
            P(),
            P(),
            P("det", None, None, None),
            P("det", "band"),
            P("det", "band"),
            P("det", "band"),
            P(None, "det", "band"),
        ),
        out_specs=P("det", "band"),
        check_vma=False,
    )
```

```python
import math

import jax
import jax.numpy as jnp
from jax import lax
from jax.experimental import pallas as pl
from jax.experimental.pallas import tpu as pltpu
from jax.sharding import PartitionSpec as P

BMAX = 8
MPRIME = 17
NPSI = 32
NPHI = 4096
BLOCK_PHI = 128
LANES = 128
ROWS = 24


def psi_tables():
    cells = jnp.arange(NPSI, dtype=jnp.int32)
    orders = jnp.arange(MPRIME, dtype=jnp.int32) - BMAX
    turns = orders[:, None] * cells[None, :] % NPSI
    angle = 2.0 * math.pi / NPSI * turns.astype(jnp.float32)
    return (jnp.cos(angle), jnp.sin(angle))


def psi_items(incoming):
    highest = lax.Precision.HIGHEST
    cos_psi, sin_psi = psi_tables()
    real_part = jnp.einsum(
        "bimn,nj->bimj", incoming[:, :, 0], cos_psi, precision=highest
    ) - jnp.einsum("bimn,nj->bimj", incoming[:, :, 1], sin_psi, precision=highest)
    imag_part = jnp.einsum(
        "bimn,nj->bimj", incoming[:, :, 0], sin_psi, precision=highest
    ) + jnp.einsum("bimn,nj->bimj", incoming[:, :, 1], cos_psi, precision=highest)
    return jnp.stack([real_part, imag_part], 2).astype(jnp.bfloat16)


def phi_table(m_values, columns):
    turns = m_values[:, None] * columns[None, :] % NPHI
    angle = 2.0 * math.pi / NPHI * turns.astype(jnp.float32)
    return jnp.concatenate([jnp.cos(angle), -jnp.sin(angle)], 0).astype(jnp.bfloat16)


def cycle_cube(samples, table, scale):
    bands, items, parts, local_orders, cells = samples.shape
    rows = jnp.transpose(samples, (1, 4, 2, 0, 3)).reshape(
        items * cells, parts * bands * local_orders
    )
    values = jnp.dot(rows, table, preferred_element_type=jnp.float32) * scale
    return values.astype(jnp.bfloat16).reshape(items, cells, table.shape[1])


def interpolate(flat_cells, block_pos, cell_phi, cell_psi, frac_phi, frac_psi):
    psi_next = (cell_psi + 1) % NPSI
    base_index = block_pos * (NPSI * BLOCK_PHI)
    low_index = base_index + cell_psi * BLOCK_PHI + cell_phi
    high_index = base_index + psi_next * BLOCK_PHI + cell_phi
    value_ll = jnp.take(flat_cells, low_index).astype(jnp.float32)
    value_lh = jnp.take(flat_cells, low_index + 1).astype(jnp.float32)
    value_hl = jnp.take(flat_cells, high_index).astype(jnp.float32)
    value_hh = jnp.take(flat_cells, high_index + 1).astype(jnp.float32)
    low_row = (1.0 - frac_phi) * value_ll + frac_phi * value_lh
    high_row = (1.0 - frac_phi) * value_hl + frac_phi * value_hh
    return (1.0 - frac_psi) * low_row + frac_psi * high_row


def by_blocks(
    sky_coeffs,
    beam_coeffs,
    wigner_panel,
    m_values,
    cycle_table,
    send_lists,
    sample_block,
    sample_phi,
    sample_psi,
    sample_frac,
):
    highest = lax.Precision.HIGHEST
    orders_all = m_values.shape[0]
    scale = 2.0 / math.sqrt(orders_all * MPRIME)
    own_band = lax.axis_index("band")
    beams = lax.all_to_all(beam_coeffs, "det", split_axis=4, concat_axis=0, tiled=True).astype(
        jnp.float32
    )
    mix_real = jnp.einsum(
        "cmk,dcnk->dmnk", sky_coeffs[:, 0], beams[:, :, 0], precision=highest
    ) + jnp.einsum("cmk,dcnk->dmnk", sky_coeffs[:, 1], beams[:, :, 1], precision=highest)
    mix_imag = jnp.einsum(
        "cmk,dcnk->dmnk", sky_coeffs[:, 1], beams[:, :, 0], precision=highest
    ) - jnp.einsum("cmk,dcnk->dmnk", sky_coeffs[:, 0], beams[:, :, 1], precision=highest)
    mixed = jnp.stack([mix_real, mix_imag], 1).astype(jnp.bfloat16)
    coeff = lax.psum_scatter(
        jnp.einsum("dsmnk,mnkr->dsmnr", mixed, wigner_panel, preferred_element_type=jnp.float32),
        "det",
        scatter_dimension=0,
        tiled=True,
    )[0]
    lists = send_lists[0]
    cycle_index = jnp.maximum(cycle_table, 0)
    table = phi_table(m_values, jnp.arange(NPHI, dtype=jnp.int32))
    payload = jnp.transpose(jnp.take(coeff, cycle_index, axis=3), (3, 4, 0, 1, 2))
    cube = cycle_cube(
        psi_items(lax.all_to_all(payload, "band", split_axis=0, concat_axis=0, tiled=True)),
        table,
        scale,
    )
    my_codes = jnp.maximum(lax.dynamic_index_in_dim(lists, own_band, 0, keepdims=False), 0)
    slot_index = my_codes // NPHI
    start_cell = my_codes % NPHI
    wrapped = jnp.concatenate([cube, cube[:, :, :BLOCK_PHI]], 2)

    def cut_block(slot_one, start_one):
        return lax.dynamic_slice(wrapped, (slot_one, 0, start_one), (1, NPSI, BLOCK_PHI))[0]

    outgoing = jax.vmap(jax.vmap(cut_block))(slot_index, start_cell)
    received = lax.all_to_all(outgoing, "band", split_axis=0, concat_axis=0, tiled=True)
    flat_cells = received.reshape(-1)
    block_pos = sample_block[0]
    values = interpolate(
        flat_cells, block_pos, sample_phi[0], sample_psi[0], sample_frac[0, 0], sample_frac[1, 0]
    )
    return values[None, :]


def smem():
    return pl.BlockSpec(memory_space=pltpu.SMEM)


def hbm():
    return pl.BlockSpec(memory_space=pltpu.HBM)


def vmem():
    return pl.BlockSpec(memory_space=pltpu.VMEM)


def cosine(turns, whole):
    folded = jnp.abs((turns & (whole - 1)) - whole // 2) - whole // 4
    x = folded.astype(jnp.float32) * (2.0 * math.pi / whole)
    y = x * x
    tail = 1.0 / 362880 - y * (1.0 / 39916800 - y * (1.0 / 6227020800))
    return x * (1.0 + y * (-1.0 / 6 + y * (1.0 / 120 + y * (-1.0 / 5040 + y * tail))))


def beam_kernel(place, source, out):
    chunk = out.shape[3] // 2
    for part in range(2):
        owner = place[0] ^ (2 * part)
        lanes = pl.ds(pl.multiple_of(owner * chunk, chunk), chunk)
        for c in range(out.shape[0]):
            block = source[c, :, :, lanes].astype(jnp.float32)
            for s in range(2):
                out[c, s, 0:MPRIME, part * chunk : (part + 1) * chunk] = block[:, s, :]
    out[:, :, MPRIME:, :] = jnp.zeros_like(out[:, :, MPRIME:, :])


def beam_copy_kernel(place, source, out, held, sem):
    copy = pltpu.make_async_copy(source, held, sem)
    copy.start()
    copy.wait()
    beam_kernel(place, held, out)


def sample_kernel(
    place, m_values, cycle_table, lists, *refs
):
    sources, (phase, low, high), (block, phi, psi, frac, sems) = refs[:4], refs[4:7], refs[7:]
    copies = [
        pltpu.make_async_copy(source, held, sems.at[i])
        for i, (source, held) in enumerate(zip(sources, (block, phi, psi, frac)))
    ]
    for copy in copies:
        copy.start()
    orders = m_values.shape[0]
    halves = phase.shape[0]
    row = lax.broadcasted_iota(jnp.int32, phase.shape[2:], 0)
    quarter = (row & 1) * (NPHI // 4)
    m = [jnp.zeros_like(row) for _ in range(halves)]
    for k in range(orders):
        half, line = divmod(k, orders // halves)
        m[half] = jnp.where(row // 2 == line, m_values[place[1] ^ k], m[half])
    for copy in copies:
        copy.wait()
    scale = 2.0 / math.sqrt(orders * MPRIME)
    band = place[1]
    blocks = block[...]
    start = jnp.zeros_like(blocks)
    cycle = jnp.zeros_like(blocks)
    sources, entries = lists.shape[:2]
    for source in range(sources):
        for entry in range(entries):
            code = jnp.maximum(lists[source, entry, band], 0)
            here = blocks == source * entries + entry
            start = jnp.where(here, code & (NPHI - 1), start)
            cycle = jnp.where(here, cycle_table[lax.div(code, NPHI), source], cycle)
    cell = psi[...]
    low[...] = cycle * NPSI + cell
    high[...] = cycle * NPSI + ((cell + 1) & (NPSI - 1))
    first = (start + phi[...]) & (NPHI - 1)
    for g in range(blocks.shape[0]):
        f = frac[0, g : g + 1, :]
        e = 1.0 - f
        for half in range(halves):
            turns = m[half] * first[g : g + 1, :] + quarter
            at = cosine(turns, NPHI).astype(jnp.bfloat16).astype(jnp.float32)
            after = cosine(turns + m[half], NPHI).astype(jnp.bfloat16).astype(jnp.float32)
            phase[half, g] = (e * at + f * after) * scale


def psi_weights(width):
    shape = (2 * ROWS, width)
    lane = lax.broadcasted_iota(jnp.int32, shape, 1) & (NPSI - 1)
    line = lax.broadcasted_iota(jnp.int32, shape, 0)
    imag = line >= ROWS
    n = jnp.where(imag, line - ROWS, line)
    turns = (n - BMAX) * lane
    c, s = cosine(turns, NPSI), cosine(turns - NPSI // 4, NPSI)
    return jnp.where(imag, -s, c), jnp.where(imag, c, s)


def rows_kernel(beam_own, beam_other, sky_own, sky_other, w_own, w_other, out):
    chunk = w_own.shape[1]
    cycles = w_own.shape[0] // MPRIME
    total = None
    for part, (sky, w) in enumerate(((sky_own, w_own), (sky_other, w_other))):
        lanes = slice(part * chunk, (part + 1) * chunk)
        pieces = []
        for beam in (beam_own, beam_other):
            real = jnp.zeros((ROWS, chunk), jnp.float32)
            imag = jnp.zeros((ROWS, chunk), jnp.float32)
            for c in range(sky.shape[0]):
                sr, si = sky[c, 0], sky[c, 1]
                br, bi = beam[c, 0, :, lanes], beam[c, 1, :, lanes]
                real += sr * br + si * bi
                imag += si * br - sr * bi
            pieces += [real, imag]
        mixed = jnp.concatenate(pieces, 0).astype(jnp.bfloat16)
        term = lax.dot_general(
            mixed, w[...], (((1,), (1,)), ((), ())), preferred_element_type=jnp.float32
        )
        total = term if total is None else total + term
    line = lax.broadcasted_iota(jnp.int32, total.shape, 0)
    column = lax.broadcasted_iota(jnp.int32, total.shape, 1)
    kept = jnp.where(lax.rem(line, ROWS) == lax.div(column, cycles), total, 0.0)
    wide = (w_own.shape[0], cycles * NPSI)
    spread = (
        lax.rem(lax.broadcasted_iota(jnp.int32, wide, 0), cycles)
        == lax.div(lax.broadcasted_iota(jnp.int32, wide, 1), NPSI)
    ).astype(jnp.bfloat16)
    coeff = jnp.zeros((total.shape[0], wide[1]), jnp.float32)
    for _ in range(3):
        piece = kept.astype(jnp.bfloat16)
        kept = kept - piece.astype(jnp.float32)
        coeff += jnp.dot(piece, spread, preferred_element_type=jnp.float32)
    weights = psi_weights(wide[1])
    for side in range(2):
        held = coeff[side * 2 * ROWS : (side + 1) * 2 * ROWS]
        for s in range(2):
            out[side, s : s + 1, :] = jnp.sum(held * weights[s], 0, keepdims=True)


def half_sum(part, phase, low, high, frac, g):
    tiles = [part[:, t : t + LANES] for t in range(0, part.shape[1], LANES)]

    def pick(index):
        index = jnp.broadcast_to(index, (part.shape[0], LANES))
        inside = index & (LANES - 1)
        value = None
        for t, tile in enumerate(tiles):
            found = jnp.take_along_axis(tile, inside, axis=1, mode="promise_in_bounds")
            value = found if value is None else jnp.where(index >= t * LANES, found, value)
        return value

    at_low, at_high = pick(low[g : g + 1, :]), pick(high[g : g + 1, :])
    return (at_low + frac[1, g : g + 1, :] * (at_high - at_low)) * phase[g]


def first_half_kernel(held, phase, low, high, frac, out):
    part = jnp.concatenate([held[k, 0].astype(jnp.float32) for k in range(held.shape[0])], 0)
    for g in range(out.shape[0]):
        out[g] = half_sum(part, phase.at[0], low, high, frac, g)


def row_sums(tiles):
    row = lax.broadcasted_iota(jnp.int32, tiles[0].shape, 0)
    for step in (1, 2, 4):
        upper = (row & step) != 0
        tiles = [
            jnp.where(upper, b, a) + pltpu.roll(jnp.where(upper, a, b), step, 0)
            for a, b in zip(tiles[::2], tiles[1::2])
        ]
    return tiles[0]


def second_half_kernel(received, first, phase, low, high, frac, out):
    part = jnp.concatenate([received[k].astype(jnp.float32) for k in range(received.shape[0])], 0)
    for g in range(0, out.shape[0], 8):
        totals = [
            first[k] + half_sum(part, phase.at[1], low, high, frac, k) for k in range(g, g + 8)
        ]
        out[g : g + 8, :] = row_sums(totals)


def call(kernel, out_shape, in_specs, flops, scratch=()):
    return pl.pallas_call(
        kernel,
        out_shape=out_shape,
        in_specs=in_specs,
        out_specs=jax.tree.map(lambda _: vmem(), out_shape),
        scratch_shapes=scratch,
        cost_estimate=pl.CostEstimate(flops=flops, bytes_accessed=1 << 20, transcendentals=0),
        compiler_params=pltpu.CompilerParams(vmem_limit_bytes=24 << 20),
    )


def by_samples(
    sky_coeffs,
    beam_coeffs,
    wigner_panel,
    m_values,
    cycle_table,
    send_lists,
    sample_block,
    sample_phi,
    sample_psi,
    sample_frac,
):
    f32 = jnp.float32
    bands = lax.axis_size("band")
    band, det = lax.axis_index("band"), lax.axis_index("det")
    place = jnp.stack([det, band])
    chunk, cycles = wigner_panel.shape[2:]
    groups = sample_block.shape[1] // LANES
    psi_width = cycles * NPSI

    sizes = (bands, lax.axis_size("det"))

    def swap(x, band_bits, det_bits):
        pairs = [
            (b * sizes[1] + d, (b ^ band_bits) * sizes[1] + (d ^ det_bits))
            for b in range(sizes[0])
            for d in range(sizes[1])
        ]
        return lax.ppermute(x, ("band", "det"), pairs)

    panel = jnp.transpose(wigner_panel[0], (0, 2, 1)).reshape(MPRIME * cycles, chunk)
    beam = jnp.transpose(beam_coeffs[0], (0, 2, 1, 3))
    panel_other = swap(panel, 0, 2)
    sky_other = swap(sky_coeffs, 0, 2)
    beam, place = lax.optimization_barrier((beam, place))
    beam_other = swap(beam, 0, 1)
    split = jax.ShapeDtypeStruct((beam.shape[0], 2, ROWS, 2 * chunk), f32)
    beam_own = call(
        beam_copy_kernel,
        split,
        [smem(), hbm()],
        1 << 22,
        [pltpu.VMEM(beam.shape, beam.dtype), pltpu.SemaphoreType.DMA],
    )(place, beam)
    beam_other = call(beam_kernel, split, [smem(), vmem()], 1 << 22)(place, beam_other)
    held = [pltpu.VMEM((groups, LANES), jnp.int32)] * 3 + [pltpu.VMEM((2, groups, LANES), f32)]
    phase, low, high = call(
        sample_kernel,
        (
            jax.ShapeDtypeStruct((2, groups, bands, LANES), f32),
            jax.ShapeDtypeStruct((groups, LANES), jnp.int32),
            jax.ShapeDtypeStruct((groups, LANES), jnp.int32),
        ),
        [smem()] * 4 + [hbm()] * 4,
        1 << 22,
        held + [pltpu.SemaphoreType.DMA((4,))],
    )(
        place,
        m_values,
        cycle_table.T,
        jnp.transpose(send_lists[0], (0, 2, 1)),
        sample_block.reshape(groups, LANES),
        sample_phi.reshape(groups, LANES),
        sample_psi.reshape(groups, LANES),
        sample_frac.reshape(2, groups, LANES),
    )
    beam_own, phase = lax.optimization_barrier((beam_own, phase))
    sums = call(rows_kernel, jax.ShapeDtypeStruct((2, 2, psi_width), f32), [vmem()] * 6, 1 << 22)(
        beam_own, beam_other, sky_coeffs, sky_other, panel, panel_other
    )
    rows = (sums + swap(sums, 0, 1)[::-1]).astype(jnp.bfloat16)
    rows_y = swap(rows, 1, 1)
    pair = jnp.stack([rows, rows_y[::-1]])
    quad = jnp.concatenate([pair, swap(pair, 2, 1)[:, ::-1]])
    rest = swap(quad[:, 1], 4, 1)
    samples = (phase, low, high, sample_frac.reshape(2, groups, LANES))
    first = call(
        first_half_kernel,
        jax.ShapeDtypeStruct((groups, bands, LANES), f32),
        [vmem()] * 5,
        1 << 22,
    )(quad, *samples)
    values = call(
        second_half_kernel, jax.ShapeDtypeStruct((groups, LANES), f32), [vmem()] * 6, 1 << 22
    )(rest, first, *samples)
    return values.reshape(1, -1)


def solution(mesh):
    def per_device(*args):
        cycles = args[2].shape[3]
        small = mesh.shape["band"] == 8 and cycles <= 8
        return (by_samples if small else by_blocks)(*args)

    return jax.shard_map(
        per_device,
        mesh=mesh,
        in_specs=(
            P(None, None, "band", "det"),
            P("det", None, None, None, None),
            P("band", None, "det", None),
            P(),
            P(),
            P("det", None, None, None),
            P("det", "band"),
            P("det", "band"),
            P("det", "band"),
            P(None, "det", "band"),
        ),
        out_specs=P("det", "band"),
        check_vma=False,
    )
```

```python
import math

import jax
import jax.numpy as jnp
from jax import lax
from jax.experimental import pallas as pl
from jax.experimental.pallas import tpu as pltpu
from jax.sharding import PartitionSpec as P

BMAX = 8
MPRIME = 17
NPSI = 32
NPHI = 4096
BLOCK_PHI = 128
LANES = 128
ROWS = 24


def psi_tables():
    cells = jnp.arange(NPSI, dtype=jnp.int32)
    orders = jnp.arange(MPRIME, dtype=jnp.int32) - BMAX
    turns = orders[:, None] * cells[None, :] % NPSI
    angle = 2.0 * math.pi / NPSI * turns.astype(jnp.float32)
    return (jnp.cos(angle), jnp.sin(angle))


def psi_items(incoming):
    highest = lax.Precision.HIGHEST
    cos_psi, sin_psi = psi_tables()
    real_part = jnp.einsum(
        "bimn,nj->bimj", incoming[:, :, 0], cos_psi, precision=highest
    ) - jnp.einsum("bimn,nj->bimj", incoming[:, :, 1], sin_psi, precision=highest)
    imag_part = jnp.einsum(
        "bimn,nj->bimj", incoming[:, :, 0], sin_psi, precision=highest
    ) + jnp.einsum("bimn,nj->bimj", incoming[:, :, 1], cos_psi, precision=highest)
    return jnp.stack([real_part, imag_part], 2).astype(jnp.bfloat16)


def phi_table(m_values, columns):
    turns = m_values[:, None] * columns[None, :] % NPHI
    angle = 2.0 * math.pi / NPHI * turns.astype(jnp.float32)
    return jnp.concatenate([jnp.cos(angle), -jnp.sin(angle)], 0).astype(jnp.bfloat16)


def cycle_cube(samples, table, scale):
    bands, items, parts, local_orders, cells = samples.shape
    rows = jnp.transpose(samples, (1, 4, 2, 0, 3)).reshape(
        items * cells, parts * bands * local_orders
    )
    values = jnp.dot(rows, table, preferred_element_type=jnp.float32) * scale
    return values.astype(jnp.bfloat16).reshape(items, cells, table.shape[1])


def interpolate(flat_cells, block_pos, cell_phi, cell_psi, frac_phi, frac_psi):
    psi_next = (cell_psi + 1) % NPSI
    base_index = block_pos * (NPSI * BLOCK_PHI)
    low_index = base_index + cell_psi * BLOCK_PHI + cell_phi
    high_index = base_index + psi_next * BLOCK_PHI + cell_phi
    value_ll = jnp.take(flat_cells, low_index).astype(jnp.float32)
    value_lh = jnp.take(flat_cells, low_index + 1).astype(jnp.float32)
    value_hl = jnp.take(flat_cells, high_index).astype(jnp.float32)
    value_hh = jnp.take(flat_cells, high_index + 1).astype(jnp.float32)
    low_row = (1.0 - frac_phi) * value_ll + frac_phi * value_lh
    high_row = (1.0 - frac_phi) * value_hl + frac_phi * value_hh
    return (1.0 - frac_psi) * low_row + frac_psi * high_row


def by_blocks(
    sky_coeffs,
    beam_coeffs,
    wigner_panel,
    m_values,
    cycle_table,
    send_lists,
    sample_block,
    sample_phi,
    sample_psi,
    sample_frac,
):
    highest = lax.Precision.HIGHEST
    orders_all = m_values.shape[0]
    scale = 2.0 / math.sqrt(orders_all * MPRIME)
    own_band = lax.axis_index("band")
    beams = lax.all_to_all(beam_coeffs, "det", split_axis=4, concat_axis=0, tiled=True).astype(
        jnp.float32
    )
    mix_real = jnp.einsum(
        "cmk,dcnk->dmnk", sky_coeffs[:, 0], beams[:, :, 0], precision=highest
    ) + jnp.einsum("cmk,dcnk->dmnk", sky_coeffs[:, 1], beams[:, :, 1], precision=highest)
    mix_imag = jnp.einsum(
        "cmk,dcnk->dmnk", sky_coeffs[:, 1], beams[:, :, 0], precision=highest
    ) - jnp.einsum("cmk,dcnk->dmnk", sky_coeffs[:, 0], beams[:, :, 1], precision=highest)
    mixed = jnp.stack([mix_real, mix_imag], 1).astype(jnp.bfloat16)
    coeff = lax.psum_scatter(
        jnp.einsum("dsmnk,mnkr->dsmnr", mixed, wigner_panel, preferred_element_type=jnp.float32),
        "det",
        scatter_dimension=0,
        tiled=True,
    )[0]
    lists = send_lists[0]
    cycle_index = jnp.maximum(cycle_table, 0)
    table = phi_table(m_values, jnp.arange(NPHI, dtype=jnp.int32))
    payload = jnp.transpose(jnp.take(coeff, cycle_index, axis=3), (3, 4, 0, 1, 2))
    cube = cycle_cube(
        psi_items(lax.all_to_all(payload, "band", split_axis=0, concat_axis=0, tiled=True)),
        table,
        scale,
    )
    my_codes = jnp.maximum(lax.dynamic_index_in_dim(lists, own_band, 0, keepdims=False), 0)
    slot_index = my_codes // NPHI
    start_cell = my_codes % NPHI
    wrapped = jnp.concatenate([cube, cube[:, :, :BLOCK_PHI]], 2)

    def cut_block(slot_one, start_one):
        return lax.dynamic_slice(wrapped, (slot_one, 0, start_one), (1, NPSI, BLOCK_PHI))[0]

    outgoing = jax.vmap(jax.vmap(cut_block))(slot_index, start_cell)
    received = lax.all_to_all(outgoing, "band", split_axis=0, concat_axis=0, tiled=True)
    flat_cells = received.reshape(-1)
    block_pos = sample_block[0]
    values = interpolate(
        flat_cells, block_pos, sample_phi[0], sample_psi[0], sample_frac[0, 0], sample_frac[1, 0]
    )
    return values[None, :]


def vmem():
    return pl.BlockSpec(memory_space=pltpu.VMEM)


def cosine(turns):
    x = jnp.abs(turns - jnp.floor(turns) - 0.5) - 0.25
    y = x * x
    total = jnp.zeros_like(x)
    for k in (11, 9, 7, 5, 3, 1):
        total = total * y + (-1.0) ** (k // 2) * (2.0 * math.pi) ** k / math.factorial(k)
    return x * total


def beam_kernel(source, out):
    chunk = out.shape[3] // 2
    det = lax.axis_index("det")
    for part in range(2):
        owner = det ^ (2 * part)
        lanes = pl.ds(pl.multiple_of(owner * chunk, chunk), chunk)
        for c in range(out.shape[0]):
            block = source[c, :, :, lanes].astype(jnp.float32)
            for s in range(2):
                out[c, s, 0:MPRIME, part * chunk : (part + 1) * chunk] = block[:, s, :]
    out[:, :, MPRIME:, :] = jnp.zeros_like(out[:, :, MPRIME:, :])


def sample_kernel(turns, table, block, phi, psi, frac, phase, *index):
    scale = 2.0 / math.sqrt(phase.shape[1] * MPRIME)
    step = turns[...]
    quarter = (lax.broadcasted_iota(jnp.int32, step.shape, 0) & 1).astype(jnp.float32) * 0.25
    starts = jnp.broadcast_to(table[0:1, :], step.shape)
    cycles = jnp.broadcast_to(table[1:2, :], step.shape)
    eight = step.shape[0]
    for h in range(0, block.shape[0], eight):
        blocks = block[h : h + eight, :]
        start = jnp.take_along_axis(starts, blocks, axis=1, mode="promise_in_bounds")
        if index:
            low, high = index
            cycle = jnp.take_along_axis(cycles, blocks, axis=1, mode="promise_in_bounds")
            cell = psi[h : h + eight, :]
            low[h : h + eight, :] = cycle * NPSI + cell
            high[h : h + eight, :] = cycle * NPSI + ((cell + 1) & (NPSI - 1))
        first = ((start + phi[h : h + eight, :]) & (NPHI - 1)).astype(jnp.float32)
        for g in range(eight):
            f = frac[0, h + g : h + g + 1, :]
            here = step * first[g : g + 1, :] + quarter
            at = cosine(here).astype(jnp.bfloat16).astype(jnp.float32)
            after = cosine(here + step).astype(jnp.bfloat16).astype(jnp.float32)
            phase[h + g] = (at + f * (after - at)) * scale


def psi_weights(width):
    shape = (2 * ROWS, width)
    lane = lax.broadcasted_iota(jnp.int32, shape, 1) & (NPSI - 1)
    line = lax.broadcasted_iota(jnp.int32, shape, 0)
    imag = line >= ROWS
    n = jnp.where(imag, line - ROWS, line)
    turns = ((n - BMAX) * lane).astype(jnp.float32) * (1.0 / NPSI)
    c, s = cosine(turns), cosine(turns - 0.25)
    return jnp.where(imag, -s, c), jnp.where(imag, c, s)


def multipole_sum(part, beams, sky, w):
    chunk = w.shape[1]
    lanes = slice(part * chunk, (part + 1) * chunk)
    pieces = []
    for beam in beams:
        real = imag = 0.0
        for c in range(sky.shape[0]):
            sr, si = sky[c, 0], sky[c, 1]
            br, bi = beam[c, 0, :, lanes], beam[c, 1, :, lanes]
            real += sr * br + si * bi
            imag += si * br - sr * bi
        pieces += [real, imag]
    mixed = jnp.concatenate(pieces, 0).astype(jnp.bfloat16)
    return lax.dot_general(
        mixed, w[...], (((1,), (1,)), ((), ())), preferred_element_type=jnp.float32
    )


def near_kernel(beam_own, beam_other, sky, w, total, weights):
    total[...] = multipole_sum(0, (beam_own, beam_other), sky, w)
    weights[0], weights[1] = psi_weights(weights.shape[2])


def rows_kernel(beam_own, beam_other, sky, w, near, weights, out):
    cycles = w.shape[0] // MPRIME
    total = near[...] + multipole_sum(1, (beam_own, beam_other), sky, w)
    line = lax.broadcasted_iota(jnp.int32, total.shape, 0)
    column = lax.broadcasted_iota(jnp.int32, total.shape, 1)
    kept = jnp.where(lax.rem(line, ROWS) == lax.div(column, cycles), total, 0.0)
    wide = (w.shape[0], weights.shape[2])
    spread = (
        lax.rem(lax.broadcasted_iota(jnp.int32, wide, 0), cycles)
        == lax.div(lax.broadcasted_iota(jnp.int32, wide, 1), NPSI)
    ).astype(jnp.bfloat16)
    coeff = jnp.zeros((total.shape[0], wide[1]), jnp.float32)
    for _ in range(3):
        piece = kept.astype(jnp.bfloat16)
        kept = kept - piece.astype(jnp.float32)
        coeff += jnp.dot(piece, spread, preferred_element_type=jnp.float32)
    for side in range(2):
        held = coeff[side * 2 * ROWS : (side + 1) * 2 * ROWS]
        for s in range(2):
            out[side, s : s + 1, :] = jnp.sum(held * weights[s], 0, keepdims=True)


def half_sum(part, phase, low, high, frac, g):
    tiles = [part[:, t : t + LANES] for t in range(0, part.shape[1], LANES)]

    def pick(index):
        index = jnp.broadcast_to(index, (part.shape[0], LANES))
        inside = index & (LANES - 1)
        value = None
        for t, tile in enumerate(tiles):
            found = jnp.take_along_axis(tile, inside, axis=1, mode="promise_in_bounds")
            value = found if value is None else jnp.where(index >= t * LANES, found, value)
        return value

    at_low, at_high = pick(low[g : g + 1, :]), pick(high[g : g + 1, :])
    return (at_low + frac[1, g : g + 1, :] * (at_high - at_low)) * phase[g]


def first_half_kernel(held, phase, low, high, frac, out):
    part = jnp.concatenate([held[k, 0].astype(jnp.float32) for k in range(held.shape[0])], 0)
    for g in range(out.shape[0]):
        out[g] = half_sum(part, phase, low, high, frac, g)


def row_sums(tiles):
    row = lax.broadcasted_iota(jnp.int32, tiles[0].shape, 0)
    for step in (1, 2, 4):
        upper = (row & step) != 0
        tiles = [
            jnp.where(upper, b, a) + pltpu.roll(jnp.where(upper, a, b), step, 0)
            for a, b in zip(tiles[::2], tiles[1::2])
        ]
    return tiles[0]


def second_half_kernel(received, first, phase, low, high, frac, out):
    part = jnp.concatenate([received[k].astype(jnp.float32) for k in range(received.shape[0])], 0)
    for g in range(0, out.shape[0], 8):
        totals = [
            first[k] + half_sum(part, phase, low, high, frac, k) for k in range(g, g + 8)
        ]
        out[g : g + 8, :] = row_sums(totals)


def call(kernel, out_shape, in_specs):
    return pl.pallas_call(
        kernel,
        out_shape=out_shape,
        in_specs=in_specs,
        out_specs=jax.tree.map(lambda _: vmem(), out_shape),
        cost_estimate=pl.CostEstimate(flops=1, bytes_accessed=1, transcendentals=0),
        compiler_params=pltpu.CompilerParams(vmem_limit_bytes=24 << 20),
    )


def by_samples(
    sky_coeffs,
    beam_coeffs,
    wigner_panel,
    m_values,
    cycle_table,
    send_lists,
    sample_block,
    sample_phi,
    sample_psi,
    sample_frac,
):
    f32 = jnp.float32
    bands = lax.axis_size("band")
    band = lax.axis_index("band")
    chunk, cycles = wigner_panel.shape[2:]
    groups = sample_block.shape[1] // LANES
    psi_width = cycles * NPSI

    sizes = (bands, lax.axis_size("det"))

    def swap(x, band_bits, det_bits):
        pairs = [
            (b * sizes[1] + d, (b ^ band_bits) * sizes[1] + (d ^ det_bits))
            for b in range(sizes[0])
            for d in range(sizes[1])
        ]
        return lax.ppermute(x, ("band", "det"), pairs)

    panel = jnp.transpose(wigner_panel[0], (0, 2, 1)).reshape(MPRIME * cycles, chunk)
    panel_other = swap(panel, 0, 2)
    sky_other = swap(sky_coeffs, 0, 2)
    beam = jnp.transpose(beam_coeffs[0], (0, 2, 1, 3))
    beam_other = swap(beam, 0, 1)
    split = jax.ShapeDtypeStruct((beam.shape[0], 2, ROWS, 2 * chunk), f32)
    beam_own = call(beam_kernel, split, [vmem()])(beam)
    beam_other = call(beam_kernel, split, [vmem()])(beam_other)
    near_sum, psi = call(
        near_kernel,
        (
            jax.ShapeDtypeStruct((4 * ROWS, MPRIME * cycles), f32),
            jax.ShapeDtypeStruct((2, 2 * ROWS, psi_width), f32),
        ),
        [vmem()] * 4,
    )(beam_own, beam_other, sky_coeffs, panel)
    sums = call(rows_kernel, jax.ShapeDtypeStruct((2, 2, psi_width), f32), [vmem()] * 6)(
        beam_own, beam_other, sky_other, panel_other, near_sum, psi
    )
    rows = (sums + swap(sums, 0, 1)[::-1]).astype(jnp.bfloat16)
    rows_y = swap(rows, 1, 1)
    here = lax.broadcasted_iota(jnp.int32, (bands, bands), 0) ^ band
    there = lax.broadcasted_iota(jnp.int32, (bands, bands), 1)
    turns = jnp.sum(jnp.where(here == there, m_values, 0), 1).astype(f32) * (1.0 / NPHI)
    turns = jnp.broadcast_to(turns.reshape(2, bands // 2, 1, 1), (2, bands // 2, 2, LANES))
    turns = turns.reshape(2, bands, LANES)
    owners = lax.broadcasted_iota(jnp.int32, send_lists.shape[1:], 1)
    codes = jnp.sum(jnp.where(owners == band, jnp.maximum(send_lists[0], 0), 0), 1)
    slots = lax.broadcasted_iota(jnp.int32, (*codes.shape, cycle_table.shape[1]), 2)
    chosen = jnp.where(slots == (codes // NPHI)[..., None], cycle_table[:, None, :], 0)
    table = jnp.stack([codes % NPHI, jnp.sum(chosen, 2)]).reshape(2, -1)
    table = jnp.pad(table, ((0, 0), (0, LANES - table.shape[1])))
    weights = jax.ShapeDtypeStruct((groups, bands, LANES), f32)
    index = jax.ShapeDtypeStruct((groups, LANES), jnp.int32)
    frac = sample_frac.reshape(2, groups, LANES)
    where = (sample_block, sample_phi, sample_psi)
    samples = (*(a.reshape(groups, LANES) for a in where), frac)
    table, _ = lax.optimization_barrier((table, rows))
    near, low, high = call(sample_kernel, (weights, index, index), [vmem()] * 6)(
        turns[0], table, *samples
    )
    rows_y, near = lax.optimization_barrier((rows_y, near))
    pair = jnp.stack([rows, rows_y[::-1]])
    pair_z = swap(pair, 2, 1)
    table, _ = lax.optimization_barrier((table, pair))
    far = call(sample_kernel, weights, [vmem()] * 6)(turns[1], table, *samples)
    pair_z, far = lax.optimization_barrier((pair_z, far))
    quad = jnp.concatenate([pair, pair_z[:, ::-1]])
    rest = swap(quad[:, 1], 4, 1)
    first = call(first_half_kernel, weights, [vmem()] * 5)(quad, near, low, high, frac)
    values = call(
        second_half_kernel, jax.ShapeDtypeStruct((groups, LANES), f32), [vmem()] * 6
    )(rest, first, far, low, high, frac)
    return values.reshape(1, -1)


def solution(mesh):
    def per_device(*args):
        cycles = args[2].shape[3]
        small = mesh.shape["band"] == 8 and cycles <= 8
        return (by_samples if small else by_blocks)(*args)

    return jax.shard_map(
        per_device,
        mesh=mesh,
        in_specs=(
            P(None, None, "band", "det"),
            P("det", None, None, None, None),
            P("band", None, "det", None),
            P(),
            P(),
            P("det", None, None, None),
            P("det", "band"),
            P("det", "band"),
            P("det", "band"),
            P(None, "det", "band"),
        ),
        out_specs=P("det", "band"),
        check_vma=False,
    )
```

```python
import math

import jax
import jax.numpy as jnp
from jax import lax
from jax.experimental import pallas as pl
from jax.experimental.pallas import tpu as pltpu
from jax.sharding import PartitionSpec as P

BMAX = 8
MPRIME = 17
NPSI = 32
NPHI = 4096
BLOCK_PHI = 128
LANES = 128
ROWS = 24


def psi_tables():
    cells = jnp.arange(NPSI, dtype=jnp.int32)
    orders = jnp.arange(MPRIME, dtype=jnp.int32) - BMAX
    turns = orders[:, None] * cells[None, :] % NPSI
    angle = 2.0 * math.pi / NPSI * turns.astype(jnp.float32)
    return (jnp.cos(angle), jnp.sin(angle))


def psi_items(incoming):
    highest = lax.Precision.HIGHEST
    cos_psi, sin_psi = psi_tables()
    real_part = jnp.einsum(
        "bimn,nj->bimj", incoming[:, :, 0], cos_psi, precision=highest
    ) - jnp.einsum("bimn,nj->bimj", incoming[:, :, 1], sin_psi, precision=highest)
    imag_part = jnp.einsum(
        "bimn,nj->bimj", incoming[:, :, 0], sin_psi, precision=highest
    ) + jnp.einsum("bimn,nj->bimj", incoming[:, :, 1], cos_psi, precision=highest)
    return jnp.stack([real_part, imag_part], 2).astype(jnp.bfloat16)


def phi_table(m_values, columns):
    turns = m_values[:, None] * columns[None, :] % NPHI
    angle = 2.0 * math.pi / NPHI * turns.astype(jnp.float32)
    return jnp.concatenate([jnp.cos(angle), -jnp.sin(angle)], 0).astype(jnp.bfloat16)


def cycle_cube(samples, table, scale):
    bands, items, parts, local_orders, cells = samples.shape
    rows = jnp.transpose(samples, (1, 4, 2, 0, 3)).reshape(
        items * cells, parts * bands * local_orders
    )
    values = jnp.dot(rows, table, preferred_element_type=jnp.float32) * scale
    return values.astype(jnp.bfloat16).reshape(items, cells, table.shape[1])


def interpolate(flat_cells, block_pos, cell_phi, cell_psi, frac_phi, frac_psi):
    psi_next = (cell_psi + 1) % NPSI
    base_index = block_pos * (NPSI * BLOCK_PHI)
    low_index = base_index + cell_psi * BLOCK_PHI + cell_phi
    high_index = base_index + psi_next * BLOCK_PHI + cell_phi
    value_ll = jnp.take(flat_cells, low_index).astype(jnp.float32)
    value_lh = jnp.take(flat_cells, low_index + 1).astype(jnp.float32)
    value_hl = jnp.take(flat_cells, high_index).astype(jnp.float32)
    value_hh = jnp.take(flat_cells, high_index + 1).astype(jnp.float32)
    low_row = (1.0 - frac_phi) * value_ll + frac_phi * value_lh
    high_row = (1.0 - frac_phi) * value_hl + frac_phi * value_hh
    return (1.0 - frac_psi) * low_row + frac_psi * high_row


def by_blocks(
    sky_coeffs,
    beam_coeffs,
    wigner_panel,
    m_values,
    cycle_table,
    send_lists,
    sample_block,
    sample_phi,
    sample_psi,
    sample_frac,
):
    highest = lax.Precision.HIGHEST
    orders_all = m_values.shape[0]
    scale = 2.0 / math.sqrt(orders_all * MPRIME)
    own_band = lax.axis_index("band")
    beams = lax.all_to_all(beam_coeffs, "det", split_axis=4, concat_axis=0, tiled=True).astype(
        jnp.float32
    )
    mix_real = jnp.einsum(
        "cmk,dcnk->dmnk", sky_coeffs[:, 0], beams[:, :, 0], precision=highest
    ) + jnp.einsum("cmk,dcnk->dmnk", sky_coeffs[:, 1], beams[:, :, 1], precision=highest)
    mix_imag = jnp.einsum(
        "cmk,dcnk->dmnk", sky_coeffs[:, 1], beams[:, :, 0], precision=highest
    ) - jnp.einsum("cmk,dcnk->dmnk", sky_coeffs[:, 0], beams[:, :, 1], precision=highest)
    mixed = jnp.stack([mix_real, mix_imag], 1).astype(jnp.bfloat16)
    coeff = lax.psum_scatter(
        jnp.einsum("dsmnk,mnkr->dsmnr", mixed, wigner_panel, preferred_element_type=jnp.float32),
        "det",
        scatter_dimension=0,
        tiled=True,
    )[0]
    lists = send_lists[0]
    cycle_index = jnp.maximum(cycle_table, 0)
    table = phi_table(m_values, jnp.arange(NPHI, dtype=jnp.int32))
    payload = jnp.transpose(jnp.take(coeff, cycle_index, axis=3), (3, 4, 0, 1, 2))
    cube = cycle_cube(
        psi_items(lax.all_to_all(payload, "band", split_axis=0, concat_axis=0, tiled=True)),
        table,
        scale,
    )
    my_codes = jnp.maximum(lax.dynamic_index_in_dim(lists, own_band, 0, keepdims=False), 0)
    slot_index = my_codes // NPHI
    start_cell = my_codes % NPHI
    wrapped = jnp.concatenate([cube, cube[:, :, :BLOCK_PHI]], 2)

    def cut_block(slot_one, start_one):
        return lax.dynamic_slice(wrapped, (slot_one, 0, start_one), (1, NPSI, BLOCK_PHI))[0]

    outgoing = jax.vmap(jax.vmap(cut_block))(slot_index, start_cell)
    received = lax.all_to_all(outgoing, "band", split_axis=0, concat_axis=0, tiled=True)
    flat_cells = received.reshape(-1)
    block_pos = sample_block[0]
    values = interpolate(
        flat_cells, block_pos, sample_phi[0], sample_psi[0], sample_frac[0, 0], sample_frac[1, 0]
    )
    return values[None, :]


def vmem():
    return pl.BlockSpec(memory_space=pltpu.VMEM)


def cosine(turns):
    x = jnp.abs(turns - jnp.floor(turns) - 0.5) - 0.25
    y = x * x
    total = jnp.zeros_like(x)
    for k in (11, 9, 7, 5, 3, 1):
        total = total * y + (-1.0) ** (k // 2) * (2.0 * math.pi) ** k / math.factorial(k)
    return x * total


def beam_kernel(source, out):
    chunk = out.shape[3] // 2
    det = lax.axis_index("det")
    for part in range(2):
        owner = det ^ (2 * part)
        lanes = pl.ds(pl.multiple_of(owner * chunk, chunk), chunk)
        for c in range(out.shape[0]):
            block = source[c, :, :, lanes].astype(jnp.float32)
            for s in range(2):
                out[c, s, 0:MPRIME, part * chunk : (part + 1) * chunk] = block[:, s, :]
    out[:, :, MPRIME:, :] = jnp.zeros_like(out[:, :, MPRIME:, :])


def sample_kernel(turns, table, block, phi, psi, frac, phase, *index):
    scale = 2.0 / math.sqrt(phase.shape[1] * MPRIME)
    step = turns[...]
    quarter = (lax.broadcasted_iota(jnp.int32, step.shape, 0) & 1).astype(jnp.float32) * 0.25
    starts = jnp.broadcast_to(table[0:1, :], step.shape)
    cycles = jnp.broadcast_to(table[1:2, :], step.shape)
    eight = step.shape[0]
    for h in range(0, block.shape[0], eight):
        blocks = block[h : h + eight, :]
        start = jnp.take_along_axis(starts, blocks, axis=1, mode="promise_in_bounds")
        if index:
            low, high = index
            cycle = jnp.take_along_axis(cycles, blocks, axis=1, mode="promise_in_bounds")
            cell = psi[h : h + eight, :]
            low[h : h + eight, :] = cycle * NPSI + cell
            high[h : h + eight, :] = cycle * NPSI + ((cell + 1) & (NPSI - 1))
        first = ((start + phi[h : h + eight, :]) & (NPHI - 1)).astype(jnp.float32)
        for g in range(eight):
            f = frac[0, h + g : h + g + 1, :]
            here = step * first[g : g + 1, :] + quarter
            at = cosine(here).astype(jnp.bfloat16).astype(jnp.float32)
            after = cosine(here + step).astype(jnp.bfloat16).astype(jnp.float32)
            phase[h + g] = (at + f * (after - at)) * scale


def pick_lanes(values, column):
    inside = column & (LANES - 1)
    picked = None
    for first in range(0, values.shape[1], LANES):
        tile = values[:, first : first + LANES]
        spare = LANES - tile.shape[1]
        if spare:
            tile = jnp.concatenate([tile, jnp.zeros((tile.shape[0], spare), tile.dtype)], 1)
        found = jnp.take_along_axis(tile, inside, axis=1, mode="promise_in_bounds")
        picked = found if picked is None else jnp.where(column >= first, found, picked)
    return picked


def psi_weights(width):
    shape = (2 * ROWS, width)
    lane = lax.broadcasted_iota(jnp.int32, shape, 1) & (NPSI - 1)
    line = lax.broadcasted_iota(jnp.int32, shape, 0)
    imag = line >= ROWS
    n = jnp.where(imag, line - ROWS, line)
    turns = ((n - BMAX) * lane).astype(jnp.float32) * (1.0 / NPSI)
    c, s = cosine(turns), cosine(turns - 0.25)
    return jnp.where(imag, -s, c), jnp.where(imag, c, s)


def multipole_sum(part, beams, sky, w):
    chunk = w.shape[1]
    lanes = slice(part * chunk, (part + 1) * chunk)
    pieces = []
    for beam in beams:
        real = imag = 0.0
        for c in range(sky.shape[0]):
            sr, si = sky[c, 0], sky[c, 1]
            br, bi = beam[c, 0, :, lanes], beam[c, 1, :, lanes]
            real += sr * br + si * bi
            imag += si * br - sr * bi
        pieces += [real, imag]
    mixed = jnp.concatenate(pieces, 0).astype(jnp.bfloat16)
    return lax.dot_general(
        mixed, w[...], (((1,), (1,)), ((), ())), preferred_element_type=jnp.float32
    )


def near_kernel(beam_own, beam_other, sky, w, total, weights):
    total[...] = multipole_sum(0, (beam_own, beam_other), sky, w)
    weights[0], weights[1] = psi_weights(weights.shape[2])


def rows_kernel(beam_own, beam_other, sky, w, near, weights, out):
    cycles = w.shape[0] // MPRIME
    total = near[...] + multipole_sum(1, (beam_own, beam_other), sky, w)
    shape = (total.shape[0], weights.shape[2])
    order = lax.rem(lax.broadcasted_iota(jnp.int32, shape, 0), ROWS)
    cycle = lax.div(lax.broadcasted_iota(jnp.int32, shape, 1), NPSI)
    column = jnp.minimum(order, MPRIME - 1) * cycles + cycle
    coeff = jnp.concatenate(
        [pick_lanes(total, column[:, t : t + LANES]) for t in range(0, shape[1], LANES)], 1
    )
    for side in range(2):
        held = coeff[side * 2 * ROWS : (side + 1) * 2 * ROWS]
        for s in range(2):
            out[side, s : s + 1, :] = jnp.sum(held * weights[s], 0, keepdims=True)


def half_sum(part, phase, low, high, frac, g):
    shape = (part.shape[0], LANES)
    at_low = pick_lanes(part, jnp.broadcast_to(low[g : g + 1, :], shape))
    at_high = pick_lanes(part, jnp.broadcast_to(high[g : g + 1, :], shape))
    return (at_low + frac[1, g : g + 1, :] * (at_high - at_low)) * phase[g]


def first_half_kernel(held, phase, low, high, frac, out):
    part = jnp.concatenate([held[k, 0].astype(jnp.float32) for k in range(held.shape[0])], 0)
    for g in range(out.shape[0]):
        out[g] = half_sum(part, phase, low, high, frac, g)


def row_sums(tiles):
    row = lax.broadcasted_iota(jnp.int32, tiles[0].shape, 0)
    for step in (1, 2, 4):
        upper = (row & step) != 0
        tiles = [
            jnp.where(upper, b, a) + pltpu.roll(jnp.where(upper, a, b), step, 0)
            for a, b in zip(tiles[::2], tiles[1::2])
        ]
    return tiles[0]


def second_half_kernel(received, first, phase, low, high, frac, out):
    part = jnp.concatenate([received[k].astype(jnp.float32) for k in range(received.shape[0])], 0)
    for g in range(0, out.shape[0], 8):
        totals = [
            first[k] + half_sum(part, phase, low, high, frac, k) for k in range(g, g + 8)
        ]
        out[g : g + 8, :] = row_sums(totals)


def call(kernel, out_shape, in_specs):
    return pl.pallas_call(
        kernel,
        out_shape=out_shape,
        in_specs=in_specs,
        out_specs=jax.tree.map(lambda _: vmem(), out_shape),
        cost_estimate=pl.CostEstimate(flops=1, bytes_accessed=1, transcendentals=0),
        compiler_params=pltpu.CompilerParams(vmem_limit_bytes=24 << 20),
    )


def by_samples(
    sky_coeffs,
    beam_coeffs,
    wigner_panel,
    m_values,
    cycle_table,
    send_lists,
    sample_block,
    sample_phi,
    sample_psi,
    sample_frac,
):
    f32 = jnp.float32
    bands = lax.axis_size("band")
    band = lax.axis_index("band")
    chunk, cycles = wigner_panel.shape[2:]
    groups = sample_block.shape[1] // LANES
    psi_width = cycles * NPSI

    sizes = (bands, lax.axis_size("det"))

    def swap(x, band_bits, det_bits):
        pairs = [
            (b * sizes[1] + d, (b ^ band_bits) * sizes[1] + (d ^ det_bits))
            for b in range(sizes[0])
            for d in range(sizes[1])
        ]
        return lax.ppermute(x, ("band", "det"), pairs)

    panel = jnp.transpose(wigner_panel[0], (0, 2, 1)).reshape(MPRIME * cycles, chunk)
    panel_other = swap(panel, 0, 2)
    sky_other = swap(sky_coeffs, 0, 2)
    beam = jnp.transpose(beam_coeffs[0], (0, 2, 1, 3))
    beam_other = swap(beam, 0, 1)
    split = jax.ShapeDtypeStruct((beam.shape[0], 2, ROWS, 2 * chunk), f32)
    beam_own = call(beam_kernel, split, [vmem()])(beam)
    beam_other = call(beam_kernel, split, [vmem()])(beam_other)
    near_sum, psi = call(
        near_kernel,
        (
            jax.ShapeDtypeStruct((4 * ROWS, MPRIME * cycles), f32),
            jax.ShapeDtypeStruct((2, 2 * ROWS, psi_width), f32),
        ),
        [vmem()] * 4,
    )(beam_own, beam_other, sky_coeffs, panel)
    sums = call(rows_kernel, jax.ShapeDtypeStruct((2, 2, psi_width), f32), [vmem()] * 6)(
        beam_own, beam_other, sky_other, panel_other, near_sum, psi
    )
    rows = (sums + swap(sums, 0, 1)[::-1]).astype(jnp.bfloat16)
    rows_y = swap(rows, 1, 1)
    here = lax.broadcasted_iota(jnp.int32, (bands, bands), 0) ^ band
    there = lax.broadcasted_iota(jnp.int32, (bands, bands), 1)
    turns = jnp.sum(jnp.where(here == there, m_values, 0), 1).astype(f32) * (1.0 / NPHI)
    turns = jnp.broadcast_to(turns.reshape(2, bands // 2, 1, 1), (2, bands // 2, 2, LANES))
    turns = turns.reshape(2, bands, LANES)
    owners = lax.broadcasted_iota(jnp.int32, send_lists.shape[1:], 1)
    codes = jnp.sum(jnp.where(owners == band, jnp.maximum(send_lists[0], 0), 0), 1)
    slots = lax.broadcasted_iota(jnp.int32, (*codes.shape, cycle_table.shape[1]), 2)
    chosen = jnp.where(slots == (codes // NPHI)[..., None], cycle_table[:, None, :], 0)
    table = jnp.stack([codes % NPHI, jnp.sum(chosen, 2)]).reshape(2, -1)
    table = jnp.pad(table, ((0, 0), (0, LANES - table.shape[1])))
    weights = jax.ShapeDtypeStruct((groups, bands, LANES), f32)
    index = jax.ShapeDtypeStruct((groups, LANES), jnp.int32)
    frac = sample_frac.reshape(2, groups, LANES)
    where = (sample_block, sample_phi, sample_psi)
    samples = (*(a.reshape(groups, LANES) for a in where), frac)
    table, _ = lax.optimization_barrier((table, rows))
    near, low, high = call(sample_kernel, (weights, index, index), [vmem()] * 6)(
        turns[0], table, *samples
    )
    rows_y, near = lax.optimization_barrier((rows_y, near))
    pair = jnp.stack([rows, rows_y[::-1]])
    pair_z = swap(pair, 2, 1)
    table, _ = lax.optimization_barrier((table, pair))
    far = call(sample_kernel, weights, [vmem()] * 6)(turns[1], table, *samples)
    pair_z, far = lax.optimization_barrier((pair_z, far))
    quad = jnp.concatenate([pair, pair_z[:, ::-1]])
    rest = swap(quad[:, 1], 4, 1)
    first = call(first_half_kernel, weights, [vmem()] * 5)(quad, near, low, high, frac)
    values = call(
        second_half_kernel, jax.ShapeDtypeStruct((groups, LANES), f32), [vmem()] * 6
    )(rest, first, far, low, high, frac)
    return values.reshape(1, -1)


def solution(mesh):
    def per_device(*args):
        cycles = args[2].shape[3]
        small = mesh.shape["band"] == 8 and cycles <= 8
        return (by_samples if small else by_blocks)(*args)

    return jax.shard_map(
        per_device,
        mesh=mesh,
        in_specs=(
            P(None, None, "band", "det"),
            P("det", None, None, None, None),
            P("band", None, "det", None),
            P(),
            P(),
            P("det", None, None, None),
            P("det", "band"),
            P("det", "band"),
            P("det", "band"),
            P(None, "det", "band"),
        ),
        out_specs=P("det", "band"),
        check_vma=False,
    )
```

```python
import math

import jax
import jax.numpy as jnp
from jax import lax
from jax.experimental import pallas as pl
from jax.experimental.pallas import tpu as pltpu
from jax.sharding import PartitionSpec as P

BMAX = 8
MPRIME = 17
NPSI = 32
NPHI = 4096
BLOCK_PHI = 128
LANES = 128
ROWS = 24


def psi_tables():
    cells = jnp.arange(NPSI, dtype=jnp.int32)
    orders = jnp.arange(MPRIME, dtype=jnp.int32) - BMAX
    turns = orders[:, None] * cells[None, :] % NPSI
    angle = 2.0 * math.pi / NPSI * turns.astype(jnp.float32)
    return (jnp.cos(angle), jnp.sin(angle))


def psi_items(incoming):
    highest = lax.Precision.HIGHEST
    cos_psi, sin_psi = psi_tables()
    real_part = jnp.einsum(
        "bimn,nj->bimj", incoming[:, :, 0], cos_psi, precision=highest
    ) - jnp.einsum("bimn,nj->bimj", incoming[:, :, 1], sin_psi, precision=highest)
    imag_part = jnp.einsum(
        "bimn,nj->bimj", incoming[:, :, 0], sin_psi, precision=highest
    ) + jnp.einsum("bimn,nj->bimj", incoming[:, :, 1], cos_psi, precision=highest)
    return jnp.stack([real_part, imag_part], 2).astype(jnp.bfloat16)


def phi_table(m_values, columns):
    turns = m_values[:, None] * columns[None, :] % NPHI
    angle = 2.0 * math.pi / NPHI * turns.astype(jnp.float32)
    return jnp.concatenate([jnp.cos(angle), -jnp.sin(angle)], 0).astype(jnp.bfloat16)


def cycle_cube(samples, table, scale):
    bands, items, parts, local_orders, cells = samples.shape
    rows = jnp.transpose(samples, (1, 4, 2, 0, 3)).reshape(
        items * cells, parts * bands * local_orders
    )
    values = jnp.dot(rows, table, preferred_element_type=jnp.float32) * scale
    return values.astype(jnp.bfloat16).reshape(items, cells, table.shape[1])


def interpolate(flat_cells, block_pos, cell_phi, cell_psi, frac_phi, frac_psi):
    psi_next = (cell_psi + 1) % NPSI
    base_index = block_pos * (NPSI * BLOCK_PHI)
    low_index = base_index + cell_psi * BLOCK_PHI + cell_phi
    high_index = base_index + psi_next * BLOCK_PHI + cell_phi
    value_ll = jnp.take(flat_cells, low_index).astype(jnp.float32)
    value_lh = jnp.take(flat_cells, low_index + 1).astype(jnp.float32)
    value_hl = jnp.take(flat_cells, high_index).astype(jnp.float32)
    value_hh = jnp.take(flat_cells, high_index + 1).astype(jnp.float32)
    low_row = (1.0 - frac_phi) * value_ll + frac_phi * value_lh
    high_row = (1.0 - frac_phi) * value_hl + frac_phi * value_hh
    return (1.0 - frac_psi) * low_row + frac_psi * high_row


def by_blocks(
    sky_coeffs,
    beam_coeffs,
    wigner_panel,
    m_values,
    cycle_table,
    send_lists,
    sample_block,
    sample_phi,
    sample_psi,
    sample_frac,
):
    highest = lax.Precision.HIGHEST
    orders_all = m_values.shape[0]
    scale = 2.0 / math.sqrt(orders_all * MPRIME)
    own_band = lax.axis_index("band")
    beams = lax.all_to_all(beam_coeffs, "det", split_axis=4, concat_axis=0, tiled=True).astype(
        jnp.float32
    )
    mix_real = jnp.einsum(
        "cmk,dcnk->dmnk", sky_coeffs[:, 0], beams[:, :, 0], precision=highest
    ) + jnp.einsum("cmk,dcnk->dmnk", sky_coeffs[:, 1], beams[:, :, 1], precision=highest)
    mix_imag = jnp.einsum(
        "cmk,dcnk->dmnk", sky_coeffs[:, 1], beams[:, :, 0], precision=highest
    ) - jnp.einsum("cmk,dcnk->dmnk", sky_coeffs[:, 0], beams[:, :, 1], precision=highest)
    mixed = jnp.stack([mix_real, mix_imag], 1).astype(jnp.bfloat16)
    coeff = lax.psum_scatter(
        jnp.einsum("dsmnk,mnkr->dsmnr", mixed, wigner_panel, preferred_element_type=jnp.float32),
        "det",
        scatter_dimension=0,
        tiled=True,
    )[0]
    lists = send_lists[0]
    cycle_index = jnp.maximum(cycle_table, 0)
    table = phi_table(m_values, jnp.arange(NPHI, dtype=jnp.int32))
    payload = jnp.transpose(jnp.take(coeff, cycle_index, axis=3), (3, 4, 0, 1, 2))
    cube = cycle_cube(
        psi_items(lax.all_to_all(payload, "band", split_axis=0, concat_axis=0, tiled=True)),
        table,
        scale,
    )
    my_codes = jnp.maximum(lax.dynamic_index_in_dim(lists, own_band, 0, keepdims=False), 0)
    slot_index = my_codes // NPHI
    start_cell = my_codes % NPHI
    wrapped = jnp.concatenate([cube, cube[:, :, :BLOCK_PHI]], 2)

    def cut_block(slot_one, start_one):
        return lax.dynamic_slice(wrapped, (slot_one, 0, start_one), (1, NPSI, BLOCK_PHI))[0]

    outgoing = jax.vmap(jax.vmap(cut_block))(slot_index, start_cell)
    received = lax.all_to_all(outgoing, "band", split_axis=0, concat_axis=0, tiled=True)
    flat_cells = received.reshape(-1)
    block_pos = sample_block[0]
    values = interpolate(
        flat_cells, block_pos, sample_phi[0], sample_psi[0], sample_frac[0, 0], sample_frac[1, 0]
    )
    return values[None, :]


def vmem():
    return pl.BlockSpec(memory_space=pltpu.VMEM)


def cosine(turns):
    x = jnp.abs(turns - jnp.floor(turns) - 0.5) - 0.25
    y = x * x
    total = jnp.zeros_like(x)
    for k in (11, 9, 7, 5, 3, 1):
        total = total * y + (-1.0) ** (k // 2) * (2.0 * math.pi) ** k / math.factorial(k)
    return x * total


def beam_kernel(source, out):
    chunk = out.shape[3] // 2
    det = lax.axis_index("det")
    for part in range(2):
        owner = det ^ (3 * part)
        lanes = pl.ds(pl.multiple_of(owner * chunk, chunk), chunk)
        for c in range(out.shape[0]):
            block = source[c, :, :, lanes].astype(jnp.float32)
            for s in range(2):
                out[c, s, 0:MPRIME, part * chunk : (part + 1) * chunk] = block[:, s, :]
    out[:, :, MPRIME:, :] = jnp.zeros_like(out[:, :, MPRIME:, :])


def sample_kernel(turns, table, block, phi, psi, frac, phase, *index):
    scale = 2.0 / math.sqrt(phase.shape[1] * MPRIME)
    step = turns[...]
    quarter = (lax.broadcasted_iota(jnp.int32, step.shape, 0) & 1).astype(jnp.float32) * 0.25
    starts = jnp.broadcast_to(table[0:1, :], step.shape)
    cycles = jnp.broadcast_to(table[1:2, :], step.shape)
    eight = step.shape[0]
    for h in range(0, block.shape[0], eight):
        blocks = block[h : h + eight, :]
        start = jnp.take_along_axis(starts, blocks, axis=1, mode="promise_in_bounds")
        if index:
            low, high = index
            cycle = jnp.take_along_axis(cycles, blocks, axis=1, mode="promise_in_bounds")
            cell = psi[h : h + eight, :]
            low[h : h + eight, :] = cycle * NPSI + cell
            high[h : h + eight, :] = cycle * NPSI + ((cell + 1) & (NPSI - 1))
        first = ((start + phi[h : h + eight, :]) & (NPHI - 1)).astype(jnp.float32)
        for g in range(eight):
            f = frac[0, h + g : h + g + 1, :]
            here = step * first[g : g + 1, :] + quarter
            at = cosine(here).astype(jnp.bfloat16).astype(jnp.float32)
            after = cosine(here + step).astype(jnp.bfloat16).astype(jnp.float32)
            phase[h + g] = (at + f * (after - at)) * scale


def pick_lanes(values, column):
    inside = column & (LANES - 1)
    picked = None
    for first in range(0, values.shape[1], LANES):
        tile = values[:, first : first + LANES]
        spare = LANES - tile.shape[1]
        if spare:
            tile = jnp.concatenate([tile, jnp.zeros((tile.shape[0], spare), tile.dtype)], 1)
        found = jnp.take_along_axis(tile, inside, axis=1, mode="promise_in_bounds")
        picked = found if picked is None else jnp.where(column >= first, found, picked)
    return picked


def psi_weights(width):
    shape = (2 * ROWS, width)
    lane = lax.broadcasted_iota(jnp.int32, shape, 1) & (NPSI - 1)
    line = lax.broadcasted_iota(jnp.int32, shape, 0)
    imag = line >= ROWS
    n = jnp.where(imag, line - ROWS, line)
    turns = ((n - BMAX) * lane).astype(jnp.float32) * (1.0 / NPSI)
    c, s = cosine(turns), cosine(turns - 0.25)
    return jnp.where(imag, -s, c), jnp.where(imag, c, s)


def multipole_sum(part, beams, sky, w):
    chunk = w.shape[1]
    lanes = slice(part * chunk, (part + 1) * chunk)
    pieces = []
    for beam in beams:
        real = imag = 0.0
        for c in range(sky.shape[0]):
            sr, si = sky[c, 0], sky[c, 1]
            br, bi = beam[c, 0, :, lanes], beam[c, 1, :, lanes]
            real += sr * br + si * bi
            imag += si * br - sr * bi
        pieces += [real, imag]
    mixed = jnp.concatenate(pieces, 0).astype(jnp.bfloat16)
    return lax.dot_general(
        mixed, w[...], (((1,), (1,)), ((), ())), preferred_element_type=jnp.float32
    )


def near_kernel(beam_own, beam_other, sky, w, total, weights):
    total[...] = multipole_sum(0, (beam_own, beam_other), sky, w)
    weights[0], weights[1] = psi_weights(weights.shape[2])


def rows_kernel(beam_own, beam_other, sky, w, near, weights, out):
    cycles = w.shape[0] // MPRIME
    total = near[...] + multipole_sum(1, (beam_own, beam_other), sky, w)
    shape = (total.shape[0], weights.shape[2])
    order = lax.rem(lax.broadcasted_iota(jnp.int32, shape, 0), ROWS)
    cycle = lax.div(lax.broadcasted_iota(jnp.int32, shape, 1), NPSI)
    column = jnp.minimum(order, MPRIME - 1) * cycles + cycle
    coeff = jnp.concatenate(
        [pick_lanes(total, column[:, t : t + LANES]) for t in range(0, shape[1], LANES)], 1
    )
    for side in range(2):
        held = coeff[side * 2 * ROWS : (side + 1) * 2 * ROWS]
        for s in range(2):
            out[side, s : s + 1, :] = jnp.sum(held * weights[s], 0, keepdims=True)


def half_sum(part, phase, low, high, frac, g):
    shape = (part.shape[0], LANES)
    at_low = pick_lanes(part, jnp.broadcast_to(low[g : g + 1, :], shape))
    at_high = pick_lanes(part, jnp.broadcast_to(high[g : g + 1, :], shape))
    return (at_low + frac[1, g : g + 1, :] * (at_high - at_low)) * phase[g]


def first_half_kernel(held, phase, low, high, frac, out):
    part = jnp.concatenate([held[k, 0].astype(jnp.float32) for k in range(held.shape[0])], 0)
    for g in range(out.shape[0]):
        out[g] = half_sum(part, phase, low, high, frac, g)


def row_sums(tiles):
    row = lax.broadcasted_iota(jnp.int32, tiles[0].shape, 0)
    for step in (1, 2, 4):
        upper = (row & step) != 0
        tiles = [
            jnp.where(upper, b, a) + pltpu.roll(jnp.where(upper, a, b), step, 0)
            for a, b in zip(tiles[::2], tiles[1::2])
        ]
    return tiles[0]


def second_half_kernel(received, first, phase, low, high, frac, out):
    part = jnp.concatenate([received[k].astype(jnp.float32) for k in range(received.shape[0])], 0)
    for g in range(0, out.shape[0], 8):
        totals = [
            first[k] + half_sum(part, phase, low, high, frac, k) for k in range(g, g + 8)
        ]
        out[g : g + 8, :] = row_sums(totals)


def call(kernel, out_shape, in_specs):
    return pl.pallas_call(
        kernel,
        out_shape=out_shape,
        in_specs=in_specs,
        out_specs=jax.tree.map(lambda _: vmem(), out_shape),
        cost_estimate=pl.CostEstimate(flops=1, bytes_accessed=1, transcendentals=0),
        compiler_params=pltpu.CompilerParams(vmem_limit_bytes=24 << 20),
    )


def by_samples(
    sky_coeffs,
    beam_coeffs,
    wigner_panel,
    m_values,
    cycle_table,
    send_lists,
    sample_block,
    sample_phi,
    sample_psi,
    sample_frac,
):
    f32 = jnp.float32
    bands = lax.axis_size("band")
    band = lax.axis_index("band")
    chunk, cycles = wigner_panel.shape[2:]
    groups = sample_block.shape[1] // LANES
    psi_width = cycles * NPSI

    sizes = (bands, lax.axis_size("det"))

    def swap(x, band_bits, det_bits):
        pairs = [
            (b * sizes[1] + d, (b ^ band_bits) * sizes[1] + (d ^ det_bits))
            for b in range(sizes[0])
            for d in range(sizes[1])
        ]
        return lax.ppermute(x, ("band", "det"), pairs)

    panel = jnp.transpose(wigner_panel[0], (0, 2, 1)).reshape(MPRIME * cycles, chunk)
    panel_other = swap(panel, 0, 3)
    sky_other = swap(sky_coeffs, 0, 3)
    beam = jnp.transpose(beam_coeffs[0], (0, 2, 1, 3))
    beam_other = swap(beam, 0, 1)
    split = jax.ShapeDtypeStruct((beam.shape[0], 2, ROWS, 2 * chunk), f32)
    beam_own = call(beam_kernel, split, [vmem()])(beam)
    beam_other = call(beam_kernel, split, [vmem()])(beam_other)
    near_sum, psi = call(
        near_kernel,
        (
            jax.ShapeDtypeStruct((4 * ROWS, MPRIME * cycles), f32),
            jax.ShapeDtypeStruct((2, 2 * ROWS, psi_width), f32),
        ),
        [vmem()] * 4,
    )(beam_own, beam_other, sky_coeffs, panel)
    sums = call(rows_kernel, jax.ShapeDtypeStruct((2, 2, psi_width), f32), [vmem()] * 6)(
        beam_own, beam_other, sky_other, panel_other, near_sum, psi
    )
    rows = (sums + swap(sums, 0, 1)[::-1]).astype(jnp.bfloat16)
    rows_y = swap(rows, 1, 1)
    here = lax.broadcasted_iota(jnp.int32, (bands, bands), 0) ^ band
    there = lax.broadcasted_iota(jnp.int32, (bands, bands), 1)
    turns = jnp.sum(jnp.where(here == there, m_values, 0), 1).astype(f32) * (1.0 / NPHI)
    turns = jnp.broadcast_to(turns.reshape(2, bands // 2, 1, 1), (2, bands // 2, 2, LANES))
    turns = turns.reshape(2, bands, LANES)
    owners = lax.broadcasted_iota(jnp.int32, send_lists.shape[1:], 1)
    codes = jnp.sum(jnp.where(owners == band, jnp.maximum(send_lists[0], 0), 0), 1)
    slots = lax.broadcasted_iota(jnp.int32, (*codes.shape, cycle_table.shape[1]), 2)
    chosen = jnp.where(slots == (codes // NPHI)[..., None], cycle_table[:, None, :], 0)
    table = jnp.stack([codes % NPHI, jnp.sum(chosen, 2)]).reshape(2, -1)
    table = jnp.pad(table, ((0, 0), (0, LANES - table.shape[1])))
    weights = jax.ShapeDtypeStruct((groups, bands, LANES), f32)
    index = jax.ShapeDtypeStruct((groups, LANES), jnp.int32)
    frac = sample_frac.reshape(2, groups, LANES)
    where = (sample_block, sample_phi, sample_psi)
    samples = (*(a.reshape(groups, LANES) for a in where), frac)
    table, _ = lax.optimization_barrier((table, rows))
    near, low, high = call(sample_kernel, (weights, index, index), [vmem()] * 6)(
        turns[0], table, *samples
    )
    rows_y, near = lax.optimization_barrier((rows_y, near))
    pair = jnp.stack([rows, rows_y[::-1]])
    pair_z = swap(pair, 2, 1)
    table, _ = lax.optimization_barrier((table, pair))
    far = call(sample_kernel, weights, [vmem()] * 6)(turns[1], table, *samples)
    pair_z, far = lax.optimization_barrier((pair_z, far))
    quad = jnp.concatenate([pair, pair_z[:, ::-1]])
    rest = swap(quad[:, 1], 4, 1)
    first = call(first_half_kernel, weights, [vmem()] * 5)(quad, near, low, high, frac)
    values = call(
        second_half_kernel, jax.ShapeDtypeStruct((groups, LANES), f32), [vmem()] * 6
    )(rest, first, far, low, high, frac)
    return values.reshape(1, -1)


def solution(mesh):
    def per_device(*args):
        cycles = args[2].shape[3]
        small = mesh.shape["band"] == 8 and cycles <= 8
        return (by_samples if small else by_blocks)(*args)

    return jax.shard_map(
        per_device,
        mesh=mesh,
        in_specs=(
            P(None, None, "band", "det"),
            P("det", None, None, None, None),
            P("band", None, "det", None),
            P(),
            P(),
            P("det", None, None, None),
            P("det", "band"),
            P("det", "band"),
            P("det", "band"),
            P(None, "det", "band"),
        ),
        out_specs=P("det", "band"),
        check_vma=False,
    )
```

```python
import functools
import math

import jax
import jax.numpy as jnp
from jax import lax
from jax.experimental import pallas as pl
from jax.experimental.pallas import tpu as pltpu
from jax.sharding import PartitionSpec as P

BMAX = 8
MPRIME = 17
NPSI = 32
NPHI = 4096
BLOCK_PHI = 128
LANES = 128
ROWS = 24


def psi_tables():
    cells = jnp.arange(NPSI, dtype=jnp.int32)
    orders = jnp.arange(MPRIME, dtype=jnp.int32) - BMAX
    turns = orders[:, None] * cells[None, :] % NPSI
    angle = 2.0 * math.pi / NPSI * turns.astype(jnp.float32)
    return (jnp.cos(angle), jnp.sin(angle))


def psi_items(incoming):
    highest = lax.Precision.HIGHEST
    cos_psi, sin_psi = psi_tables()
    real_part = jnp.einsum(
        "bimn,nj->bimj", incoming[:, :, 0], cos_psi, precision=highest
    ) - jnp.einsum("bimn,nj->bimj", incoming[:, :, 1], sin_psi, precision=highest)
    imag_part = jnp.einsum(
        "bimn,nj->bimj", incoming[:, :, 0], sin_psi, precision=highest
    ) + jnp.einsum("bimn,nj->bimj", incoming[:, :, 1], cos_psi, precision=highest)
    return jnp.stack([real_part, imag_part], 2).astype(jnp.bfloat16)


def phi_table(m_values, columns):
    turns = m_values[:, None] * columns[None, :] % NPHI
    angle = 2.0 * math.pi / NPHI * turns.astype(jnp.float32)
    return jnp.concatenate([jnp.cos(angle), -jnp.sin(angle)], 0).astype(jnp.bfloat16)


def cycle_cube(samples, table, scale):
    bands, items, parts, local_orders, cells = samples.shape
    rows = jnp.transpose(samples, (1, 4, 2, 0, 3)).reshape(
        items * cells, parts * bands * local_orders
    )
    values = jnp.dot(rows, table, preferred_element_type=jnp.float32) * scale
    return values.astype(jnp.bfloat16).reshape(items, cells, table.shape[1])


def interpolate(flat_cells, block_pos, cell_phi, cell_psi, frac_phi, frac_psi):
    psi_next = (cell_psi + 1) % NPSI
    base_index = block_pos * (NPSI * BLOCK_PHI)
    low_index = base_index + cell_psi * BLOCK_PHI + cell_phi
    high_index = base_index + psi_next * BLOCK_PHI + cell_phi
    value_ll = jnp.take(flat_cells, low_index).astype(jnp.float32)
    value_lh = jnp.take(flat_cells, low_index + 1).astype(jnp.float32)
    value_hl = jnp.take(flat_cells, high_index).astype(jnp.float32)
    value_hh = jnp.take(flat_cells, high_index + 1).astype(jnp.float32)
    low_row = (1.0 - frac_phi) * value_ll + frac_phi * value_lh
    high_row = (1.0 - frac_phi) * value_hl + frac_phi * value_hh
    return (1.0 - frac_psi) * low_row + frac_psi * high_row


def by_blocks(
    sky_coeffs,
    beam_coeffs,
    wigner_panel,
    m_values,
    cycle_table,
    send_lists,
    sample_block,
    sample_phi,
    sample_psi,
    sample_frac,
):
    highest = lax.Precision.HIGHEST
    orders_all = m_values.shape[0]
    scale = 2.0 / math.sqrt(orders_all * MPRIME)
    own_band = lax.axis_index("band")
    beams = lax.all_to_all(beam_coeffs, "det", split_axis=4, concat_axis=0, tiled=True).astype(
        jnp.float32
    )
    mix_real = jnp.einsum(
        "cmk,dcnk->dmnk", sky_coeffs[:, 0], beams[:, :, 0], precision=highest
    ) + jnp.einsum("cmk,dcnk->dmnk", sky_coeffs[:, 1], beams[:, :, 1], precision=highest)
    mix_imag = jnp.einsum(
        "cmk,dcnk->dmnk", sky_coeffs[:, 1], beams[:, :, 0], precision=highest
    ) - jnp.einsum("cmk,dcnk->dmnk", sky_coeffs[:, 0], beams[:, :, 1], precision=highest)
    mixed = jnp.stack([mix_real, mix_imag], 1).astype(jnp.bfloat16)
    coeff = lax.psum_scatter(
        jnp.einsum("dsmnk,mnkr->dsmnr", mixed, wigner_panel, preferred_element_type=jnp.float32),
        "det",
        scatter_dimension=0,
        tiled=True,
    )[0]
    lists = send_lists[0]
    cycle_index = jnp.maximum(cycle_table, 0)
    table = phi_table(m_values, jnp.arange(NPHI, dtype=jnp.int32))
    payload = jnp.transpose(jnp.take(coeff, cycle_index, axis=3), (3, 4, 0, 1, 2))
    cube = cycle_cube(
        psi_items(lax.all_to_all(payload, "band", split_axis=0, concat_axis=0, tiled=True)),
        table,
        scale,
    )
    my_codes = jnp.maximum(lax.dynamic_index_in_dim(lists, own_band, 0, keepdims=False), 0)
    slot_index = my_codes // NPHI
    start_cell = my_codes % NPHI
    wrapped = jnp.concatenate([cube, cube[:, :, :BLOCK_PHI]], 2)

    def cut_block(slot_one, start_one):
        return lax.dynamic_slice(wrapped, (slot_one, 0, start_one), (1, NPSI, BLOCK_PHI))[0]

    outgoing = jax.vmap(jax.vmap(cut_block))(slot_index, start_cell)
    received = lax.all_to_all(outgoing, "band", split_axis=0, concat_axis=0, tiled=True)
    flat_cells = received.reshape(-1)
    block_pos = sample_block[0]
    values = interpolate(
        flat_cells, block_pos, sample_phi[0], sample_psi[0], sample_frac[0, 0], sample_frac[1, 0]
    )
    return values[None, :]


def vmem():
    return pl.BlockSpec(memory_space=pltpu.VMEM)


def cosine(turns):
    x = jnp.abs(turns - jnp.floor(turns) - 0.5) - 0.25
    y = x * x
    total = jnp.zeros_like(x)
    for k in (11, 9, 7, 5, 3, 1):
        total = total * y + (-1.0) ** (k // 2) * (2.0 * math.pi) ** k / math.factorial(k)
    return x * total


def beam_kernel(source, out):
    chunk = out.shape[3] // 2
    det = lax.axis_index("det")
    for part in range(2):
        owner = det ^ (3 * part)
        lanes = pl.ds(pl.multiple_of(owner * chunk, chunk), chunk)
        for c in range(out.shape[0]):
            block = source[c, :, :, lanes].astype(jnp.float32)
            for s in range(2):
                out[c, s, 0:MPRIME, part * chunk : (part + 1) * chunk] = block[:, s, :]
    out[:, :, MPRIME:, :] = jnp.zeros_like(out[:, :, MPRIME:, :])


def own_lanes(values, column):
    spare = jnp.zeros((values.shape[0], LANES - values.shape[1]), values.dtype)
    wide = jnp.concatenate([values, spare], 1)
    return jnp.take_along_axis(wide, column, axis=1, mode="promise_in_bounds")


def sample_kernel(half, orders, cycles, lists, block, phi, psi, frac, phase, *index):
    scale = 2.0 / math.sqrt(phase.shape[1] * MPRIME)
    band = lax.axis_index("band")
    eight = phase.shape[1]
    row = lax.broadcasted_iota(jnp.int32, (eight, LANES), 0)
    orders = jnp.broadcast_to(orders[...], (eight, orders.shape[1]))
    order = own_lanes(orders, band ^ (half * (eight // 2) + row // 2))
    step = order.astype(jnp.float32) * (1.0 / NPHI)
    quarter = (row & 1).astype(jnp.float32) * 0.25
    sources, entries = lists.shape[:2]
    codes = jnp.concatenate([lists[source] for source in range(sources)], 0)
    codes = jnp.maximum(own_lanes(codes, jnp.full((codes.shape[0], LANES), band)), 0)
    for h in range(0, block.shape[0], eight):
        blocks = block[h : h + eight, :]
        start = jnp.zeros_like(blocks)
        cycle = jnp.zeros_like(blocks)
        for entry in range(sources * entries):
            code = codes[entry : entry + 1, :]
            here = blocks == entry
            start = jnp.where(here, code & (NPHI - 1), start)
            if index:
                source = entry // entries
                for slot in range(cycles.shape[0]):
                    kept = here & (code >= slot * NPHI)
                    cycle = jnp.where(kept, cycles[slot : slot + 1, source : source + 1], cycle)
        if index:
            low, high = index
            cell = psi[h : h + eight, :]
            low[h : h + eight, :] = cycle * NPSI + cell
            high[h : h + eight, :] = cycle * NPSI + ((cell + 1) & (NPSI - 1))
        first = ((start + phi[h : h + eight, :]) & (NPHI - 1)).astype(jnp.float32)
        for g in range(eight):
            f = frac[0, h + g : h + g + 1, :]
            here = step * first[g : g + 1, :] + quarter
            at = cosine(here).astype(jnp.bfloat16).astype(jnp.float32)
            after = cosine(here + step).astype(jnp.bfloat16).astype(jnp.float32)
            phase[h + g] = (at + f * (after - at)) * scale


def pick_lanes(values, column):
    inside = column & (LANES - 1)
    picked = None
    for first in range(0, values.shape[1], LANES):
        tile = values[:, first : first + LANES]
        spare = LANES - tile.shape[1]
        if spare:
            tile = jnp.concatenate([tile, jnp.zeros((tile.shape[0], spare), tile.dtype)], 1)
        found = jnp.take_along_axis(tile, inside, axis=1, mode="promise_in_bounds")
        picked = found if picked is None else jnp.where(column >= first, found, picked)
    return picked


def psi_weights(width):
    shape = (2 * ROWS, width)
    lane = lax.broadcasted_iota(jnp.int32, shape, 1) & (NPSI - 1)
    line = lax.broadcasted_iota(jnp.int32, shape, 0)
    imag = line >= ROWS
    n = jnp.where(imag, line - ROWS, line)
    turns = ((n - BMAX) * lane).astype(jnp.float32) * (1.0 / NPSI)
    c, s = cosine(turns), cosine(turns - 0.25)
    return jnp.where(imag, -s, c), jnp.where(imag, c, s)


def multipole_sum(part, beams, sky, w):
    chunk = w.shape[1]
    lanes = slice(part * chunk, (part + 1) * chunk)
    pieces = []
    for beam in beams:
        real = imag = 0.0
        for c in range(sky.shape[0]):
            sr, si = sky[c, 0], sky[c, 1]
            br, bi = beam[c, 0, :, lanes], beam[c, 1, :, lanes]
            real += sr * br + si * bi
            imag += si * br - sr * bi
        pieces += [real, imag]
    mixed = jnp.concatenate(pieces, 0).astype(jnp.bfloat16)
    return lax.dot_general(
        mixed, w[...], (((1,), (1,)), ((), ())), preferred_element_type=jnp.float32
    )


def near_kernel(beam_own, beam_other, sky, w, total, weights):
    total[...] = multipole_sum(0, (beam_own, beam_other), sky, w)
    weights[0], weights[1] = psi_weights(weights.shape[2])


def rows_kernel(beam_own, beam_other, sky, w, near, weights, out):
    cycles = w.shape[0] // MPRIME
    total = near[...] + multipole_sum(1, (beam_own, beam_other), sky, w)
    shape = (total.shape[0], weights.shape[2])
    order = lax.rem(lax.broadcasted_iota(jnp.int32, shape, 0), ROWS)
    cycle = lax.div(lax.broadcasted_iota(jnp.int32, shape, 1), NPSI)
    column = jnp.minimum(order, MPRIME - 1) * cycles + cycle
    coeff = jnp.concatenate(
        [pick_lanes(total, column[:, t : t + LANES]) for t in range(0, shape[1], LANES)], 1
    )
    for side in range(2):
        held = coeff[side * 2 * ROWS : (side + 1) * 2 * ROWS]
        for s in range(2):
            out[side, s : s + 1, :] = jnp.sum(held * weights[s], 0, keepdims=True)


def half_sum(part, phase, low, high, frac, g):
    shape = (part.shape[0], LANES)
    at_low = pick_lanes(part, jnp.broadcast_to(low[g : g + 1, :], shape))
    at_high = pick_lanes(part, jnp.broadcast_to(high[g : g + 1, :], shape))
    return (at_low + frac[1, g : g + 1, :] * (at_high - at_low)) * phase[g]


def first_half_kernel(held, phase, low, high, frac, out):
    part = jnp.concatenate([held[k, 0].astype(jnp.float32) for k in range(held.shape[0])], 0)
    for g in range(out.shape[0]):
        out[g] = half_sum(part, phase, low, high, frac, g)


def row_sums(tiles):
    row = lax.broadcasted_iota(jnp.int32, tiles[0].shape, 0)
    for step in (1, 2, 4):
        upper = (row & step) != 0
        tiles = [
            jnp.where(upper, b, a) + pltpu.roll(jnp.where(upper, a, b), step, 0)
            for a, b in zip(tiles[::2], tiles[1::2])
        ]
    return tiles[0]


def second_half_kernel(received, first, phase, low, high, frac, out):
    part = jnp.concatenate([received[k].astype(jnp.float32) for k in range(received.shape[0])], 0)
    for g in range(0, out.shape[0], 8):
        totals = [
            first[k] + half_sum(part, phase, low, high, frac, k) for k in range(g, g + 8)
        ]
        out[g : g + 8, :] = row_sums(totals)


def call(kernel, out_shape, in_specs):
    return pl.pallas_call(
        kernel,
        out_shape=out_shape,
        in_specs=in_specs,
        out_specs=jax.tree.map(lambda _: vmem(), out_shape),
        cost_estimate=pl.CostEstimate(flops=1, bytes_accessed=1, transcendentals=0),
        compiler_params=pltpu.CompilerParams(vmem_limit_bytes=24 << 20),
    )


def by_samples(
    sky_coeffs,
    beam_coeffs,
    wigner_panel,
    m_values,
    cycle_table,
    send_lists,
    sample_block,
    sample_phi,
    sample_psi,
    sample_frac,
):
    f32 = jnp.float32
    bands = lax.axis_size("band")
    chunk, cycles = wigner_panel.shape[2:]
    groups = sample_block.shape[1] // LANES
    psi_width = cycles * NPSI

    sizes = (bands, lax.axis_size("det"))

    def swap(x, band_bits, det_bits):
        pairs = [
            (b * sizes[1] + d, (b ^ band_bits) * sizes[1] + (d ^ det_bits))
            for b in range(sizes[0])
            for d in range(sizes[1])
        ]
        return lax.ppermute(x, ("band", "det"), pairs)

    panel = jnp.transpose(wigner_panel[0], (0, 2, 1)).reshape(MPRIME * cycles, chunk)
    panel_other = swap(panel, 0, 3)
    sky_other = swap(sky_coeffs, 0, 3)
    beam = jnp.transpose(beam_coeffs[0], (0, 2, 1, 3))
    beam_other = swap(beam, 0, 1)
    split = jax.ShapeDtypeStruct((beam.shape[0], 2, ROWS, 2 * chunk), f32)
    beam_own = call(beam_kernel, split, [vmem()])(beam)
    beam_other = call(beam_kernel, split, [vmem()])(beam_other)
    near_sum, psi = call(
        near_kernel,
        (
            jax.ShapeDtypeStruct((4 * ROWS, MPRIME * cycles), f32),
            jax.ShapeDtypeStruct((2, 2 * ROWS, psi_width), f32),
        ),
        [vmem()] * 4,
    )(beam_own, beam_other, sky_coeffs, panel)
    sums = call(rows_kernel, jax.ShapeDtypeStruct((2, 2, psi_width), f32), [vmem()] * 6)(
        beam_own, beam_other, sky_other, panel_other, near_sum, psi
    )
    rows = (sums + swap(sums, 0, 1)[::-1]).astype(jnp.bfloat16)
    rows_y = swap(rows, 1, 1)
    weights = jax.ShapeDtypeStruct((groups, bands, LANES), f32)
    index = jax.ShapeDtypeStruct((groups, LANES), jnp.int32)
    frac = sample_frac.reshape(2, groups, LANES)
    where = (sample_block, sample_phi, sample_psi)
    lists = (m_values.reshape(1, -1), cycle_table.T, jnp.transpose(send_lists[0], (0, 2, 1)))
    samples = (*lists, *(a.reshape(groups, LANES) for a in where), frac)
    late, _ = lax.optimization_barrier((samples[0], rows))
    near, low, high = call(
        functools.partial(sample_kernel, 0), (weights, index, index), [vmem()] * 7
    )(late, *samples[1:])
    rows_y, near = lax.optimization_barrier((rows_y, near))
    pair = jnp.stack([rows, rows_y[::-1]])
    pair_z = swap(pair, 2, 1)
    late, _ = lax.optimization_barrier((samples[0], pair))
    far = call(functools.partial(sample_kernel, 1), weights, [vmem()] * 7)(late, *samples[1:])
    pair_z, far = lax.optimization_barrier((pair_z, far))
    quad = jnp.concatenate([pair, pair_z[:, ::-1]])
    rest = swap(quad[:, 1], 4, 1)
    first = call(first_half_kernel, weights, [vmem()] * 5)(quad, near, low, high, frac)
    values = call(
        second_half_kernel, jax.ShapeDtypeStruct((groups, LANES), f32), [vmem()] * 6
    )(rest, first, far, low, high, frac)
    return values.reshape(1, -1)


def solution(mesh):
    def per_device(*args):
        cycles = args[2].shape[3]
        small = mesh.shape["band"] == 8 and cycles <= 8
        return (by_samples if small else by_blocks)(*args)

    return jax.shard_map(
        per_device,
        mesh=mesh,
        in_specs=(
            P(None, None, "band", "det"),
            P("det", None, None, None, None),
            P("band", None, "det", None),
            P(),
            P(),
            P("det", None, None, None),
            P("det", "band"),
            P("det", "band"),
            P("det", "band"),
            P(None, "det", "band"),
        ),
        out_specs=P("det", "band"),
        check_vma=False,
    )
```

```python
import functools
import math

import jax
import jax.numpy as jnp
from jax import lax
from jax.experimental import pallas as pl
from jax.experimental.pallas import tpu as pltpu
from jax.sharding import PartitionSpec as P

BMAX = 8
MPRIME = 17
NPSI = 32
NPHI = 4096
BLOCK_PHI = 128
LANES = 128
ROWS = 24


def psi_tables():
    cells = jnp.arange(NPSI, dtype=jnp.int32)
    orders = jnp.arange(MPRIME, dtype=jnp.int32) - BMAX
    turns = orders[:, None] * cells[None, :] % NPSI
    angle = 2.0 * math.pi / NPSI * turns.astype(jnp.float32)
    return (jnp.cos(angle), jnp.sin(angle))


def psi_items(incoming):
    highest = lax.Precision.HIGHEST
    cos_psi, sin_psi = psi_tables()
    real_part = jnp.einsum(
        "bimn,nj->bimj", incoming[:, :, 0], cos_psi, precision=highest
    ) - jnp.einsum("bimn,nj->bimj", incoming[:, :, 1], sin_psi, precision=highest)
    imag_part = jnp.einsum(
        "bimn,nj->bimj", incoming[:, :, 0], sin_psi, precision=highest
    ) + jnp.einsum("bimn,nj->bimj", incoming[:, :, 1], cos_psi, precision=highest)
    return jnp.stack([real_part, imag_part], 2).astype(jnp.bfloat16)


def phi_table(m_values, columns):
    turns = m_values[:, None] * columns[None, :] % NPHI
    angle = 2.0 * math.pi / NPHI * turns.astype(jnp.float32)
    return jnp.concatenate([jnp.cos(angle), -jnp.sin(angle)], 0).astype(jnp.bfloat16)


def cycle_cube(samples, table, scale):
    bands, items, parts, local_orders, cells = samples.shape
    rows = jnp.transpose(samples, (1, 4, 2, 0, 3)).reshape(
        items * cells, parts * bands * local_orders
    )
    values = jnp.dot(rows, table, preferred_element_type=jnp.float32) * scale
    return values.astype(jnp.bfloat16).reshape(items, cells, table.shape[1])


def interpolate(flat_cells, block_pos, cell_phi, cell_psi, frac_phi, frac_psi):
    psi_next = (cell_psi + 1) % NPSI
    base_index = block_pos * (NPSI * BLOCK_PHI)
    low_index = base_index + cell_psi * BLOCK_PHI + cell_phi
    high_index = base_index + psi_next * BLOCK_PHI + cell_phi
    value_ll = jnp.take(flat_cells, low_index).astype(jnp.float32)
    value_lh = jnp.take(flat_cells, low_index + 1).astype(jnp.float32)
    value_hl = jnp.take(flat_cells, high_index).astype(jnp.float32)
    value_hh = jnp.take(flat_cells, high_index + 1).astype(jnp.float32)
    low_row = (1.0 - frac_phi) * value_ll + frac_phi * value_lh
    high_row = (1.0 - frac_phi) * value_hl + frac_phi * value_hh
    return (1.0 - frac_psi) * low_row + frac_psi * high_row


def by_blocks(
    sky_coeffs,
    beam_coeffs,
    wigner_panel,
    m_values,
    cycle_table,
    send_lists,
    sample_block,
    sample_phi,
    sample_psi,
    sample_frac,
):
    highest = lax.Precision.HIGHEST
    orders_all = m_values.shape[0]
    scale = 2.0 / math.sqrt(orders_all * MPRIME)
    own_band = lax.axis_index("band")
    beams = lax.all_to_all(beam_coeffs, "det", split_axis=4, concat_axis=0, tiled=True).astype(
        jnp.float32
    )
    mix_real = jnp.einsum(
        "cmk,dcnk->dmnk", sky_coeffs[:, 0], beams[:, :, 0], precision=highest
    ) + jnp.einsum("cmk,dcnk->dmnk", sky_coeffs[:, 1], beams[:, :, 1], precision=highest)
    mix_imag = jnp.einsum(
        "cmk,dcnk->dmnk", sky_coeffs[:, 1], beams[:, :, 0], precision=highest
    ) - jnp.einsum("cmk,dcnk->dmnk", sky_coeffs[:, 0], beams[:, :, 1], precision=highest)
    mixed = jnp.stack([mix_real, mix_imag], 1).astype(jnp.bfloat16)
    coeff = lax.psum_scatter(
        jnp.einsum("dsmnk,mnkr->dsmnr", mixed, wigner_panel, preferred_element_type=jnp.float32),
        "det",
        scatter_dimension=0,
        tiled=True,
    )[0]
    lists = send_lists[0]
    cycle_index = jnp.maximum(cycle_table, 0)
    table = phi_table(m_values, jnp.arange(NPHI, dtype=jnp.int32))
    payload = jnp.transpose(jnp.take(coeff, cycle_index, axis=3), (3, 4, 0, 1, 2))
    cube = cycle_cube(
        psi_items(lax.all_to_all(payload, "band", split_axis=0, concat_axis=0, tiled=True)),
        table,
        scale,
    )
    my_codes = jnp.maximum(lax.dynamic_index_in_dim(lists, own_band, 0, keepdims=False), 0)
    slot_index = my_codes // NPHI
    start_cell = my_codes % NPHI
    wrapped = jnp.concatenate([cube, cube[:, :, :BLOCK_PHI]], 2)

    def cut_block(slot_one, start_one):
        return lax.dynamic_slice(wrapped, (slot_one, 0, start_one), (1, NPSI, BLOCK_PHI))[0]

    outgoing = jax.vmap(jax.vmap(cut_block))(slot_index, start_cell)
    received = lax.all_to_all(outgoing, "band", split_axis=0, concat_axis=0, tiled=True)
    flat_cells = received.reshape(-1)
    block_pos = sample_block[0]
    values = interpolate(
        flat_cells, block_pos, sample_phi[0], sample_psi[0], sample_frac[0, 0], sample_frac[1, 0]
    )
    return values[None, :]


def vmem():
    return pl.BlockSpec(memory_space=pltpu.VMEM)


def cosine(turns):
    x = jnp.abs(turns - jnp.floor(turns) - 0.5) - 0.25
    y = x * x
    total = jnp.zeros_like(x)
    for k in (11, 9, 7, 5, 3, 1):
        total = total * y + (-1.0) ** (k // 2) * (2.0 * math.pi) ** k / math.factorial(k)
    return x * total


def beam_kernel(source, out):
    chunk = out.shape[3] // 2
    det = lax.axis_index("det")
    for part in range(2):
        owner = det ^ (3 * part)
        lanes = pl.ds(pl.multiple_of(owner * chunk, chunk), chunk)
        for c in range(out.shape[0]):
            block = source[c, :, :, lanes].astype(jnp.float32)
            for s in range(2):
                out[c, s, 0:MPRIME, part * chunk : (part + 1) * chunk] = block[:, s, :]
    out[:, :, MPRIME:, :] = jnp.zeros_like(out[:, :, MPRIME:, :])


def own_lanes(values, column):
    spare = jnp.zeros((values.shape[0], LANES - values.shape[1]), values.dtype)
    wide = jnp.concatenate([values, spare], 1)
    return jnp.take_along_axis(wide, column, axis=1, mode="promise_in_bounds")


def sample_kernel(half, orders, cycles, lists, block, phi, psi, frac, phase, *index):
    scale = 2.0 / math.sqrt(phase.shape[1] * MPRIME)
    band = lax.axis_index("band")
    eight = phase.shape[1]
    row = lax.broadcasted_iota(jnp.int32, (eight, LANES), 0)
    orders = jnp.broadcast_to(orders[...], (eight, orders.shape[1]))
    order = own_lanes(orders, band ^ (half * (eight // 2) + row // 2))
    step = order.astype(jnp.float32) * (1.0 / NPHI)
    quarter = (row & 1).astype(jnp.float32) * 0.25
    sources, entries = lists.shape[:2]
    codes = jnp.concatenate([lists[source] for source in range(sources)], 0)
    codes = jnp.maximum(own_lanes(codes, jnp.full((codes.shape[0], LANES), band)), 0)
    for h in range(0, block.shape[0], eight):
        blocks = block[h : h + eight, :]
        start = jnp.zeros_like(blocks)
        cycle = jnp.zeros_like(blocks)
        for entry in range(sources * entries):
            code = codes[entry : entry + 1, :]
            here = blocks == entry
            start = jnp.where(here, code & (NPHI - 1), start)
            if index:
                source = entry // entries
                for slot in range(cycles.shape[0]):
                    kept = here & (code >= slot * NPHI)
                    cycle = jnp.where(kept, cycles[slot : slot + 1, source : source + 1], cycle)
        if index:
            low, high = index
            cell = psi[h : h + eight, :]
            low[h : h + eight, :] = cycle * NPSI + cell
            high[h : h + eight, :] = cycle * NPSI + ((cell + 1) & (NPSI - 1))
        first = ((start + phi[h : h + eight, :]) & (NPHI - 1)).astype(jnp.float32)
        for g in range(eight):
            f = frac[0, h + g : h + g + 1, :]
            here = step * first[g : g + 1, :] + quarter
            at = cosine(here).astype(jnp.bfloat16).astype(jnp.float32)
            after = cosine(here + step).astype(jnp.bfloat16).astype(jnp.float32)
            phase[h + g] = (at + f * (after - at)) * scale


def pick_lanes(values, column):
    inside = column & (LANES - 1)
    picked = None
    for first in range(0, values.shape[1], LANES):
        tile = values[:, first : first + LANES]
        spare = LANES - tile.shape[1]
        if spare:
            tile = jnp.concatenate([tile, jnp.zeros((tile.shape[0], spare), tile.dtype)], 1)
        found = jnp.take_along_axis(tile, inside, axis=1, mode="promise_in_bounds")
        picked = found if picked is None else jnp.where(column >= first, found, picked)
    return picked


def psi_weights(width):
    shape = (2 * ROWS, width)
    lane = lax.broadcasted_iota(jnp.int32, shape, 1) & (NPSI - 1)
    line = lax.broadcasted_iota(jnp.int32, shape, 0)
    imag = line >= ROWS
    n = jnp.where(imag, line - ROWS, line)
    turns = ((n - BMAX) * lane).astype(jnp.float32) * (1.0 / NPSI)
    c, s = cosine(turns), cosine(turns - 0.25)
    return jnp.where(imag, -s, c), jnp.where(imag, c, s)


def multipole_sum(part, beams, sky, w):
    chunk = w.shape[1]
    lanes = slice(part * chunk, (part + 1) * chunk)
    pieces = []
    for beam in beams:
        real = imag = 0.0
        for c in range(sky.shape[0]):
            sr, si = sky[c, 0], sky[c, 1]
            br, bi = beam[c, 0, :, lanes], beam[c, 1, :, lanes]
            real += sr * br + si * bi
            imag += si * br - sr * bi
        pieces += [real, imag]
    mixed = jnp.concatenate(pieces, 0).astype(jnp.bfloat16)
    return lax.dot_general(
        mixed, w[...], (((1,), (1,)), ((), ())), preferred_element_type=jnp.float32
    )


def near_kernel(beam_own, beam_other, sky, w, total, weights):
    total[...] = multipole_sum(0, (beam_own, beam_other), sky, w)
    weights[0], weights[1] = psi_weights(weights.shape[2])


def rows_kernel(beam_own, beam_other, sky, w, near, weights, out):
    cycles = w.shape[0] // MPRIME
    total = near[...] + multipole_sum(1, (beam_own, beam_other), sky, w)
    shape = (total.shape[0], weights.shape[2])
    order = lax.rem(lax.broadcasted_iota(jnp.int32, shape, 0), ROWS)
    cycle = lax.div(lax.broadcasted_iota(jnp.int32, shape, 1), NPSI)
    column = jnp.minimum(order, MPRIME - 1) * cycles + cycle
    coeff = jnp.concatenate(
        [pick_lanes(total, column[:, t : t + LANES]) for t in range(0, shape[1], LANES)], 1
    )
    for side in range(2):
        held = coeff[side * 2 * ROWS : (side + 1) * 2 * ROWS]
        for s in range(2):
            out[side, s : s + 1, :] = jnp.sum(held * weights[s], 0, keepdims=True)


def half_sum(part, phase, low, high, frac, g):
    shape = (part.shape[0], LANES)
    at_low = pick_lanes(part, jnp.broadcast_to(low[g : g + 1, :], shape))
    at_high = pick_lanes(part, jnp.broadcast_to(high[g : g + 1, :], shape))
    return (at_low + frac[1, g : g + 1, :] * (at_high - at_low)) * phase[g]


def first_half_kernel(held, received, phase, low, high, frac, out):
    parts = (held[0, 0], held[1, 1], received[0, 1], received[1, 0])
    part = jnp.concatenate([rows.astype(jnp.float32) for rows in parts], 0)
    for g in range(out.shape[0]):
        out[g] = half_sum(part, phase, low, high, frac, g)


def row_sums(tiles):
    row = lax.broadcasted_iota(jnp.int32, tiles[0].shape, 0)
    for step in (1, 2, 4):
        upper = (row & step) != 0
        tiles = [
            jnp.where(upper, b, a) + pltpu.roll(jnp.where(upper, a, b), step, 0)
            for a, b in zip(tiles[::2], tiles[1::2])
        ]
    return tiles[0]


def second_half_kernel(received, first, phase, low, high, frac, out):
    part = jnp.concatenate([received[k].astype(jnp.float32) for k in range(received.shape[0])], 0)
    for g in range(0, out.shape[0], 8):
        totals = [
            first[k] + half_sum(part, phase, low, high, frac, k) for k in range(g, g + 8)
        ]
        out[g : g + 8, :] = row_sums(totals)


def call(kernel, out_shape, in_specs):
    return pl.pallas_call(
        kernel,
        out_shape=out_shape,
        in_specs=in_specs,
        out_specs=jax.tree.map(lambda _: vmem(), out_shape),
        cost_estimate=pl.CostEstimate(flops=1, bytes_accessed=1, transcendentals=0),
        compiler_params=pltpu.CompilerParams(vmem_limit_bytes=24 << 20),
    )


def by_samples(
    sky_coeffs,
    beam_coeffs,
    wigner_panel,
    m_values,
    cycle_table,
    send_lists,
    sample_block,
    sample_phi,
    sample_psi,
    sample_frac,
):
    f32 = jnp.float32
    bands = lax.axis_size("band")
    chunk, cycles = wigner_panel.shape[2:]
    groups = sample_block.shape[1] // LANES
    psi_width = cycles * NPSI

    sizes = (bands, lax.axis_size("det"))

    def swap(x, band_bits, det_bits):
        pairs = [
            (b * sizes[1] + d, (b ^ band_bits) * sizes[1] + (d ^ det_bits))
            for b in range(sizes[0])
            for d in range(sizes[1])
        ]
        return lax.ppermute(x, ("band", "det"), pairs)

    panel = jnp.transpose(wigner_panel[0], (0, 2, 1)).reshape(MPRIME * cycles, chunk)
    panel_other = swap(panel, 0, 3)
    sky_other = swap(sky_coeffs, 0, 3)
    beam = jnp.transpose(beam_coeffs[0], (0, 2, 1, 3))
    beam_other = swap(beam, 0, 1)
    split = jax.ShapeDtypeStruct((beam.shape[0], 2, ROWS, 2 * chunk), f32)
    beam_own = call(beam_kernel, split, [vmem()])(beam)
    beam_other = call(beam_kernel, split, [vmem()])(beam_other)
    near_sum, psi = call(
        near_kernel,
        (
            jax.ShapeDtypeStruct((4 * ROWS, MPRIME * cycles), f32),
            jax.ShapeDtypeStruct((2, 2 * ROWS, psi_width), f32),
        ),
        [vmem()] * 4,
    )(beam_own, beam_other, sky_coeffs, panel)
    sums = call(rows_kernel, jax.ShapeDtypeStruct((2, 2, psi_width), f32), [vmem()] * 6)(
        beam_own, beam_other, sky_other, panel_other, near_sum, psi
    )
    rows = (sums + swap(sums, 0, 1)[::-1]).astype(jnp.bfloat16)
    rows_y = swap(rows, 1, 1)
    weights = jax.ShapeDtypeStruct((groups, bands, LANES), f32)
    index = jax.ShapeDtypeStruct((groups, LANES), jnp.int32)
    frac = sample_frac.reshape(2, groups, LANES)
    where = (sample_block, sample_phi, sample_psi)
    lists = (m_values.reshape(1, -1), cycle_table.T, jnp.transpose(send_lists[0], (0, 2, 1)))
    samples = (*lists, *(a.reshape(groups, LANES) for a in where), frac)
    late, _ = lax.optimization_barrier((samples[0], rows))
    near, low, high = call(
        functools.partial(sample_kernel, 0), (weights, index, index), [vmem()] * 7
    )(late, *samples[1:])
    rows_y, near = lax.optimization_barrier((rows_y, near))
    pair = jnp.stack([rows, rows_y])
    pair_z = swap(pair, 2, 1)
    late, _ = lax.optimization_barrier((samples[0], pair))
    far = call(functools.partial(sample_kernel, 1), weights, [vmem()] * 7)(late, *samples[1:])
    pair_z, far = lax.optimization_barrier((pair_z, far))
    rest = swap(jnp.stack([pair[0, 1], pair[1, 0], pair_z[0, 0], pair_z[1, 1]]), 4, 1)
    first = call(first_half_kernel, weights, [vmem()] * 6)(pair, pair_z, near, low, high, frac)
    values = call(
        second_half_kernel, jax.ShapeDtypeStruct((groups, LANES), f32), [vmem()] * 6
    )(rest, first, far, low, high, frac)
    return values.reshape(1, -1)


def solution(mesh):
    def per_device(*args):
        cycles = args[2].shape[3]
        small = mesh.shape["band"] == 8 and cycles <= 8
        return (by_samples if small else by_blocks)(*args)

    return jax.shard_map(
        per_device,
        mesh=mesh,
        in_specs=(
            P(None, None, "band", "det"),
            P("det", None, None, None, None),
            P("band", None, "det", None),
            P(),
            P(),
            P("det", None, None, None),
            P("det", "band"),
            P("det", "band"),
            P("det", "band"),
            P(None, "det", "band"),
        ),
        out_specs=P("det", "band"),
        check_vma=False,
    )
```

```python
import functools
import math

import jax
import jax.numpy as jnp
from jax import lax
from jax.experimental import pallas as pl
from jax.experimental.pallas import tpu as pltpu
from jax.sharding import PartitionSpec as P

BMAX = 8
MPRIME = 17
NPSI = 32
NPHI = 4096
BLOCK_PHI = 128
LANES = 128
ROWS = 24


def psi_tables():
    cells = jnp.arange(NPSI, dtype=jnp.int32)
    orders = jnp.arange(MPRIME, dtype=jnp.int32) - BMAX
    turns = orders[:, None] * cells[None, :] % NPSI
    angle = 2.0 * math.pi / NPSI * turns.astype(jnp.float32)
    return (jnp.cos(angle), jnp.sin(angle))


def psi_items(incoming):
    highest = lax.Precision.HIGHEST
    cos_psi, sin_psi = psi_tables()
    real_part = jnp.einsum(
        "bimn,nj->bimj", incoming[:, :, 0], cos_psi, precision=highest
    ) - jnp.einsum("bimn,nj->bimj", incoming[:, :, 1], sin_psi, precision=highest)
    imag_part = jnp.einsum(
        "bimn,nj->bimj", incoming[:, :, 0], sin_psi, precision=highest
    ) + jnp.einsum("bimn,nj->bimj", incoming[:, :, 1], cos_psi, precision=highest)
    return jnp.stack([real_part, imag_part], 2).astype(jnp.bfloat16)


def phi_table(m_values, columns):
    turns = m_values[:, None] * columns[None, :] % NPHI
    angle = 2.0 * math.pi / NPHI * turns.astype(jnp.float32)
    return jnp.concatenate([jnp.cos(angle), -jnp.sin(angle)], 0).astype(jnp.bfloat16)


def cycle_cube(samples, table, scale):
    bands, items, parts, local_orders, cells = samples.shape
    rows = jnp.transpose(samples, (1, 4, 2, 0, 3)).reshape(
        items * cells, parts * bands * local_orders
    )
    values = jnp.dot(rows, table, preferred_element_type=jnp.float32) * scale
    return values.astype(jnp.bfloat16).reshape(items, cells, table.shape[1])


def interpolate(flat_cells, block_pos, cell_phi, cell_psi, frac_phi, frac_psi):
    psi_next = (cell_psi + 1) % NPSI
    base_index = block_pos * (NPSI * BLOCK_PHI)
    low_index = base_index + cell_psi * BLOCK_PHI + cell_phi
    high_index = base_index + psi_next * BLOCK_PHI + cell_phi
    value_ll = jnp.take(flat_cells, low_index).astype(jnp.float32)
    value_lh = jnp.take(flat_cells, low_index + 1).astype(jnp.float32)
    value_hl = jnp.take(flat_cells, high_index).astype(jnp.float32)
    value_hh = jnp.take(flat_cells, high_index + 1).astype(jnp.float32)
    low_row = (1.0 - frac_phi) * value_ll + frac_phi * value_lh
    high_row = (1.0 - frac_phi) * value_hl + frac_phi * value_hh
    return (1.0 - frac_psi) * low_row + frac_psi * high_row


def by_blocks(
    sky_coeffs,
    beam_coeffs,
    wigner_panel,
    m_values,
    cycle_table,
    send_lists,
    sample_block,
    sample_phi,
    sample_psi,
    sample_frac,
):
    highest = lax.Precision.HIGHEST
    orders_all = m_values.shape[0]
    scale = 2.0 / math.sqrt(orders_all * MPRIME)
    own_band = lax.axis_index("band")
    beams = lax.all_to_all(beam_coeffs, "det", split_axis=4, concat_axis=0, tiled=True).astype(
        jnp.float32
    )
    mix_real = jnp.einsum(
        "cmk,dcnk->dmnk", sky_coeffs[:, 0], beams[:, :, 0], precision=highest
    ) + jnp.einsum("cmk,dcnk->dmnk", sky_coeffs[:, 1], beams[:, :, 1], precision=highest)
    mix_imag = jnp.einsum(
        "cmk,dcnk->dmnk", sky_coeffs[:, 1], beams[:, :, 0], precision=highest
    ) - jnp.einsum("cmk,dcnk->dmnk", sky_coeffs[:, 0], beams[:, :, 1], precision=highest)
    mixed = jnp.stack([mix_real, mix_imag], 1).astype(jnp.bfloat16)
    coeff = lax.psum_scatter(
        jnp.einsum("dsmnk,mnkr->dsmnr", mixed, wigner_panel, preferred_element_type=jnp.float32),
        "det",
        scatter_dimension=0,
        tiled=True,
    )[0]
    lists = send_lists[0]
    cycle_index = jnp.maximum(cycle_table, 0)
    table = phi_table(m_values, jnp.arange(NPHI, dtype=jnp.int32))
    payload = jnp.transpose(jnp.take(coeff, cycle_index, axis=3), (3, 4, 0, 1, 2))
    cube = cycle_cube(
        psi_items(lax.all_to_all(payload, "band", split_axis=0, concat_axis=0, tiled=True)),
        table,
        scale,
    )
    my_codes = jnp.maximum(lax.dynamic_index_in_dim(lists, own_band, 0, keepdims=False), 0)
    slot_index = my_codes // NPHI
    start_cell = my_codes % NPHI
    wrapped = jnp.concatenate([cube, cube[:, :, :BLOCK_PHI]], 2)

    def cut_block(slot_one, start_one):
        return lax.dynamic_slice(wrapped, (slot_one, 0, start_one), (1, NPSI, BLOCK_PHI))[0]

    outgoing = jax.vmap(jax.vmap(cut_block))(slot_index, start_cell)
    received = lax.all_to_all(outgoing, "band", split_axis=0, concat_axis=0, tiled=True)
    flat_cells = received.reshape(-1)
    block_pos = sample_block[0]
    values = interpolate(
        flat_cells, block_pos, sample_phi[0], sample_psi[0], sample_frac[0, 0], sample_frac[1, 0]
    )
    return values[None, :]


def vmem():
    return pl.BlockSpec(memory_space=pltpu.VMEM)


def cosine(turns):
    x = jnp.abs(turns - jnp.floor(turns) - 0.5) - 0.25
    y = x * x
    total = jnp.zeros_like(x)
    for k in (11, 9, 7, 5, 3, 1):
        total = total * y + (-1.0) ** (k // 2) * (2.0 * math.pi) ** k / math.factorial(k)
    return x * total


def beam_kernel(source, out):
    chunk = out.shape[3] // 2
    det = lax.axis_index("det")
    for part in range(2):
        owner = det ^ (3 * part)
        lanes = pl.ds(pl.multiple_of(owner * chunk, chunk), chunk)
        for c in range(out.shape[0]):
            block = source[c, :, :, lanes].astype(jnp.float32)
            for s in range(2):
                out[c, s, 0:MPRIME, part * chunk : (part + 1) * chunk] = block[:, s, :]
    out[:, :, MPRIME:, :] = jnp.zeros_like(out[:, :, MPRIME:, :])


def own_lanes(values, column):
    spare = jnp.zeros((values.shape[0], LANES - values.shape[1]), values.dtype)
    wide = jnp.concatenate([values, spare], 1)
    return jnp.take_along_axis(wide, column, axis=1, mode="promise_in_bounds")


def sample_kernel(half, orders, cycles, lists, block, phi, psi, frac, phase, *index):
    scale = 2.0 / math.sqrt(phase.shape[1] * MPRIME)
    band = lax.axis_index("band")
    eight = phase.shape[1]
    row = lax.broadcasted_iota(jnp.int32, (eight, LANES), 0)
    orders = jnp.broadcast_to(orders[...], (eight, orders.shape[1]))
    order = own_lanes(orders, band ^ (half * (eight // 2) + row // 2))
    step = order.astype(jnp.float32) * (1.0 / NPHI)
    quarter = (row & 1).astype(jnp.float32) * 0.25
    sources, entries = lists.shape[:2]
    codes = jnp.concatenate([lists[source] for source in range(sources)], 0)
    codes = jnp.maximum(own_lanes(codes, jnp.full((codes.shape[0], LANES), band)), 0)
    for h in range(0, block.shape[0], eight):
        blocks = block[h : h + eight, :]
        start = jnp.zeros_like(blocks)
        cycle = jnp.zeros_like(blocks)
        for entry in range(sources * entries):
            code = codes[entry : entry + 1, :]
            here = blocks == entry
            start = jnp.where(here, code & (NPHI - 1), start)
            if index:
                source = entry // entries
                for slot in range(cycles.shape[0]):
                    kept = here & (code >= slot * NPHI)
                    cycle = jnp.where(kept, cycles[slot : slot + 1, source : source + 1], cycle)
        if index:
            index[0][h : h + eight, :] = cycle * NPSI + psi[h : h + eight, :]
        first = ((start + phi[h : h + eight, :]) & (NPHI - 1)).astype(jnp.float32)
        for g in range(eight):
            f = frac[0, h + g : h + g + 1, :]
            here = step * first[g : g + 1, :] + quarter
            at = cosine(here).astype(jnp.bfloat16).astype(jnp.float32)
            after = cosine(here + step).astype(jnp.bfloat16).astype(jnp.float32)
            phase[h + g] = (at + f * (after - at)) * scale


def pick_lanes(values, column):
    inside = column & (LANES - 1)
    picked = None
    for first in range(0, values.shape[1], LANES):
        tile = values[:, first : first + LANES]
        spare = LANES - tile.shape[1]
        if spare:
            tile = jnp.concatenate([tile, jnp.zeros((tile.shape[0], spare), tile.dtype)], 1)
        found = jnp.take_along_axis(tile, inside, axis=1, mode="promise_in_bounds")
        picked = found if picked is None else jnp.where(column >= first, found, picked)
    return picked


def psi_weights(width):
    shape = (2 * ROWS, width)
    lane = lax.broadcasted_iota(jnp.int32, shape, 1) & (NPSI - 1)
    line = lax.broadcasted_iota(jnp.int32, shape, 0)
    imag = line >= ROWS
    n = jnp.where(imag, line - ROWS, line)
    turns = ((n - BMAX) * lane).astype(jnp.float32) * (1.0 / NPSI)
    c, s = cosine(turns), cosine(turns - 0.25)
    return jnp.where(imag, -s, c), jnp.where(imag, c, s)


def multipole_sum(part, beams, sky, w):
    chunk = w.shape[1]
    lanes = slice(part * chunk, (part + 1) * chunk)
    pieces = []
    for beam in beams:
        real = imag = 0.0
        for c in range(sky.shape[0]):
            sr, si = sky[c, 0], sky[c, 1]
            br, bi = beam[c, 0, :, lanes], beam[c, 1, :, lanes]
            real += sr * br + si * bi
            imag += si * br - sr * bi
        pieces += [real, imag]
    mixed = jnp.concatenate(pieces, 0).astype(jnp.bfloat16)
    return lax.dot_general(
        mixed, w[...], (((1,), (1,)), ((), ())), preferred_element_type=jnp.float32
    )


def near_kernel(beam_own, beam_other, sky, w, total, weights):
    total[...] = multipole_sum(0, (beam_own, beam_other), sky, w)
    weights[0], weights[1] = psi_weights(weights.shape[2])


def rows_kernel(beam_own, beam_other, sky, w, near, weights, out):
    cycles = w.shape[0] // MPRIME
    total = near[...] + multipole_sum(1, (beam_own, beam_other), sky, w)
    shape = (total.shape[0], weights.shape[2])
    order = lax.rem(lax.broadcasted_iota(jnp.int32, shape, 0), ROWS)
    cycle = lax.div(lax.broadcasted_iota(jnp.int32, shape, 1), NPSI)
    column = jnp.minimum(order, MPRIME - 1) * cycles + cycle
    coeff = jnp.concatenate(
        [pick_lanes(total, column[:, t : t + LANES]) for t in range(0, shape[1], LANES)], 1
    )
    for side in range(2):
        held = coeff[side * 2 * ROWS : (side + 1) * 2 * ROWS]
        for s in range(2):
            out[side, s : s + 1, :] = jnp.sum(held * weights[s], 0, keepdims=True)


def to_next_psi(part):
    width = part.shape[1]
    last = lax.broadcasted_iota(jnp.int32, part.shape, 1) & (NPSI - 1) == NPSI - 1
    after = jnp.where(last, pltpu.roll(part, NPSI - 1, 1), pltpu.roll(part, width - 1, 1))
    return after - part


def half_sum(part, change, phase, low, frac, g):
    at = jnp.broadcast_to(low[g : g + 1, :], (part.shape[0], LANES))
    value = pick_lanes(part, at) + frac[1, g : g + 1, :] * pick_lanes(change, at)
    return value * phase[g]


def first_half_kernel(held, received, phase, low, frac, out):
    parts = (held[0, 0], held[1, 1], received[0, 1], received[1, 0])
    part = jnp.concatenate([rows.astype(jnp.float32) for rows in parts], 0)
    change = to_next_psi(part)
    for g in range(out.shape[0]):
        out[g] = half_sum(part, change, phase, low, frac, g)


def row_sums(tiles):
    row = lax.broadcasted_iota(jnp.int32, tiles[0].shape, 0)
    for step in (1, 2, 4):
        upper = (row & step) != 0
        tiles = [
            jnp.where(upper, b, a) + pltpu.roll(jnp.where(upper, a, b), step, 0)
            for a, b in zip(tiles[::2], tiles[1::2])
        ]
    return tiles[0]


def second_half_kernel(received, first, phase, low, frac, out):
    part = jnp.concatenate([received[k].astype(jnp.float32) for k in range(received.shape[0])], 0)
    change = to_next_psi(part)
    for g in range(0, out.shape[0], 8):
        totals = [
            first[k] + half_sum(part, change, phase, low, frac, k) for k in range(g, g + 8)
        ]
        out[g : g + 8, :] = row_sums(totals)


def call(kernel, out_shape, in_specs):
    return pl.pallas_call(
        kernel,
        out_shape=out_shape,
        in_specs=in_specs,
        out_specs=jax.tree.map(lambda _: vmem(), out_shape),
        cost_estimate=pl.CostEstimate(flops=1, bytes_accessed=1, transcendentals=0),
        compiler_params=pltpu.CompilerParams(vmem_limit_bytes=24 << 20),
    )


def by_samples(
    sky_coeffs,
    beam_coeffs,
    wigner_panel,
    m_values,
    cycle_table,
    send_lists,
    sample_block,
    sample_phi,
    sample_psi,
    sample_frac,
):
    f32 = jnp.float32
    bands = lax.axis_size("band")
    chunk, cycles = wigner_panel.shape[2:]
    groups = sample_block.shape[1] // LANES
    psi_width = cycles * NPSI

    sizes = (bands, lax.axis_size("det"))

    def swap(x, band_bits, det_bits):
        pairs = [
            (b * sizes[1] + d, (b ^ band_bits) * sizes[1] + (d ^ det_bits))
            for b in range(sizes[0])
            for d in range(sizes[1])
        ]
        return lax.ppermute(x, ("band", "det"), pairs)

    panel = jnp.transpose(wigner_panel[0], (0, 2, 1)).reshape(MPRIME * cycles, chunk)
    panel_other = swap(panel, 0, 3)
    sky_other = swap(sky_coeffs, 0, 3)
    beam = jnp.transpose(beam_coeffs[0], (0, 2, 1, 3))
    beam_other = swap(beam, 0, 1)
    split = jax.ShapeDtypeStruct((beam.shape[0], 2, ROWS, 2 * chunk), f32)
    beam_own = call(beam_kernel, split, [vmem()])(beam)
    beam_other = call(beam_kernel, split, [vmem()])(beam_other)
    near_sum, psi = call(
        near_kernel,
        (
            jax.ShapeDtypeStruct((4 * ROWS, MPRIME * cycles), f32),
            jax.ShapeDtypeStruct((2, 2 * ROWS, psi_width), f32),
        ),
        [vmem()] * 4,
    )(beam_own, beam_other, sky_coeffs, panel)
    sums = call(rows_kernel, jax.ShapeDtypeStruct((2, 2, psi_width), f32), [vmem()] * 6)(
        beam_own, beam_other, sky_other, panel_other, near_sum, psi
    )
    rows = (sums + swap(sums, 0, 1)[::-1]).astype(jnp.bfloat16)
    rows_y = swap(rows, 1, 1)
    weights = jax.ShapeDtypeStruct((groups, bands, LANES), f32)
    index = jax.ShapeDtypeStruct((groups, LANES), jnp.int32)
    frac = sample_frac.reshape(2, groups, LANES)
    where = (sample_block, sample_phi, sample_psi)
    lists = (m_values.reshape(1, -1), cycle_table.T, jnp.transpose(send_lists[0], (0, 2, 1)))
    samples = (*lists, *(a.reshape(groups, LANES) for a in where), frac)
    late, _ = lax.optimization_barrier((samples[0], rows))
    near, low = call(
        functools.partial(sample_kernel, 0), (weights, index), [vmem()] * 7
    )(late, *samples[1:])
    rows_y, near = lax.optimization_barrier((rows_y, near))
    pair = jnp.stack([rows, rows_y])
    pair_z = swap(pair, 2, 1)
    late, _ = lax.optimization_barrier((samples[0], pair))
    far = call(functools.partial(sample_kernel, 1), weights, [vmem()] * 7)(late, *samples[1:])
    pair_z, far = lax.optimization_barrier((pair_z, far))
    rest = swap(jnp.stack([pair[0, 1], pair[1, 0], pair_z[0, 0], pair_z[1, 1]]), 4, 1)
    first = call(first_half_kernel, weights, [vmem()] * 5)(pair, pair_z, near, low, frac)
    values = call(
        second_half_kernel, jax.ShapeDtypeStruct((groups, LANES), f32), [vmem()] * 5
    )(rest, first, far, low, frac)
    return values.reshape(1, -1)


def solution(mesh):
    def per_device(*args):
        cycles = args[2].shape[3]
        small = mesh.shape["band"] == 8 and cycles <= 8
        return (by_samples if small else by_blocks)(*args)

    return jax.shard_map(
        per_device,
        mesh=mesh,
        in_specs=(
            P(None, None, "band", "det"),
            P("det", None, None, None, None),
            P("band", None, "det", None),
            P(),
            P(),
            P("det", None, None, None),
            P("det", "band"),
            P("det", "band"),
            P("det", "band"),
            P(None, "det", "band"),
        ),
        out_specs=P("det", "band"),
        check_vma=False,
    )
```

```python
import functools
import math

import jax
import jax.numpy as jnp
from jax import lax
from jax.experimental import pallas as pl
from jax.experimental.pallas import tpu as pltpu
from jax.sharding import PartitionSpec as P

BMAX = 8
MPRIME = 17
NPSI = 32
NPHI = 4096
BLOCK_PHI = 128
LANES = 128
ROWS = 24


def psi_tables():
    cells = jnp.arange(NPSI, dtype=jnp.int32)
    orders = jnp.arange(MPRIME, dtype=jnp.int32) - BMAX
    turns = orders[:, None] * cells[None, :] % NPSI
    angle = 2.0 * math.pi / NPSI * turns.astype(jnp.float32)
    return (jnp.cos(angle), jnp.sin(angle))


def psi_items(incoming):
    highest = lax.Precision.HIGHEST
    cos_psi, sin_psi = psi_tables()
    real_part = jnp.einsum(
        "bimn,nj->bimj", incoming[:, :, 0], cos_psi, precision=highest
    ) - jnp.einsum("bimn,nj->bimj", incoming[:, :, 1], sin_psi, precision=highest)
    imag_part = jnp.einsum(
        "bimn,nj->bimj", incoming[:, :, 0], sin_psi, precision=highest
    ) + jnp.einsum("bimn,nj->bimj", incoming[:, :, 1], cos_psi, precision=highest)
    return jnp.stack([real_part, imag_part], 2).astype(jnp.bfloat16)


def phi_table(m_values, columns):
    turns = m_values[:, None] * columns[None, :] % NPHI
    angle = 2.0 * math.pi / NPHI * turns.astype(jnp.float32)
    return jnp.concatenate([jnp.cos(angle), -jnp.sin(angle)], 0).astype(jnp.bfloat16)


def cycle_cube(samples, table, scale):
    bands, items, parts, local_orders, cells = samples.shape
    rows = jnp.transpose(samples, (1, 4, 2, 0, 3)).reshape(
        items * cells, parts * bands * local_orders
    )
    values = jnp.dot(rows, table, preferred_element_type=jnp.float32) * scale
    return values.astype(jnp.bfloat16).reshape(items, cells, table.shape[1])


def interpolate(flat_cells, block_pos, cell_phi, cell_psi, frac_phi, frac_psi):
    psi_next = (cell_psi + 1) % NPSI
    base_index = block_pos * (NPSI * BLOCK_PHI)
    low_index = base_index + cell_psi * BLOCK_PHI + cell_phi
    high_index = base_index + psi_next * BLOCK_PHI + cell_phi
    value_ll = jnp.take(flat_cells, low_index).astype(jnp.float32)
    value_lh = jnp.take(flat_cells, low_index + 1).astype(jnp.float32)
    value_hl = jnp.take(flat_cells, high_index).astype(jnp.float32)
    value_hh = jnp.take(flat_cells, high_index + 1).astype(jnp.float32)
    low_row = (1.0 - frac_phi) * value_ll + frac_phi * value_lh
    high_row = (1.0 - frac_phi) * value_hl + frac_phi * value_hh
    return (1.0 - frac_psi) * low_row + frac_psi * high_row


def by_blocks(
    sky_coeffs,
    beam_coeffs,
    wigner_panel,
    m_values,
    cycle_table,
    send_lists,
    sample_block,
    sample_phi,
    sample_psi,
    sample_frac,
):
    highest = lax.Precision.HIGHEST
    orders_all = m_values.shape[0]
    scale = 2.0 / math.sqrt(orders_all * MPRIME)
    own_band = lax.axis_index("band")
    beams = lax.all_to_all(beam_coeffs, "det", split_axis=4, concat_axis=0, tiled=True).astype(
        jnp.float32
    )
    mix_real = jnp.einsum(
        "cmk,dcnk->dmnk", sky_coeffs[:, 0], beams[:, :, 0], precision=highest
    ) + jnp.einsum("cmk,dcnk->dmnk", sky_coeffs[:, 1], beams[:, :, 1], precision=highest)
    mix_imag = jnp.einsum(
        "cmk,dcnk->dmnk", sky_coeffs[:, 1], beams[:, :, 0], precision=highest
    ) - jnp.einsum("cmk,dcnk->dmnk", sky_coeffs[:, 0], beams[:, :, 1], precision=highest)
    mixed = jnp.stack([mix_real, mix_imag], 1).astype(jnp.bfloat16)
    coeff = lax.psum_scatter(
        jnp.einsum("dsmnk,mnkr->dsmnr", mixed, wigner_panel, preferred_element_type=jnp.float32),
        "det",
        scatter_dimension=0,
        tiled=True,
    )[0]
    lists = send_lists[0]
    cycle_index = jnp.maximum(cycle_table, 0)
    table = phi_table(m_values, jnp.arange(NPHI, dtype=jnp.int32))
    payload = jnp.transpose(jnp.take(coeff, cycle_index, axis=3), (3, 4, 0, 1, 2))
    cube = cycle_cube(
        psi_items(lax.all_to_all(payload, "band", split_axis=0, concat_axis=0, tiled=True)),
        table,
        scale,
    )
    my_codes = jnp.maximum(lax.dynamic_index_in_dim(lists, own_band, 0, keepdims=False), 0)
    slot_index = my_codes // NPHI
    start_cell = my_codes % NPHI
    wrapped = jnp.concatenate([cube, cube[:, :, :BLOCK_PHI]], 2)

    def cut_block(slot_one, start_one):
        return lax.dynamic_slice(wrapped, (slot_one, 0, start_one), (1, NPSI, BLOCK_PHI))[0]

    outgoing = jax.vmap(jax.vmap(cut_block))(slot_index, start_cell)
    received = lax.all_to_all(outgoing, "band", split_axis=0, concat_axis=0, tiled=True)
    flat_cells = received.reshape(-1)
    block_pos = sample_block[0]
    values = interpolate(
        flat_cells, block_pos, sample_phi[0], sample_psi[0], sample_frac[0, 0], sample_frac[1, 0]
    )
    return values[None, :]


def vmem():
    return pl.BlockSpec(memory_space=pltpu.VMEM)


def cosine(turns):
    x = jnp.abs(turns - jnp.floor(turns) - 0.5) - 0.25
    y = x * x
    total = jnp.zeros_like(x)
    for k in (11, 9, 7, 5, 3, 1):
        total = total * y + (-1.0) ** (k // 2) * (2.0 * math.pi) ** k / math.factorial(k)
    return x * total


def beam_kernel(source, out):
    chunk = out.shape[3] // 2
    det = lax.axis_index("det")
    for part in range(2):
        owner = det ^ (3 * part)
        lanes = pl.ds(pl.multiple_of(owner * chunk, chunk), chunk)
        for c in range(out.shape[0]):
            block = source[c, :, :, lanes].astype(jnp.float32)
            for s in range(2):
                out[c, s, 0:MPRIME, part * chunk : (part + 1) * chunk] = block[:, s, :]
    out[:, :, MPRIME:, :] = jnp.zeros_like(out[:, :, MPRIME:, :])


def own_lanes(values, column):
    spare = jnp.zeros((values.shape[0], LANES - values.shape[1]), values.dtype)
    wide = jnp.concatenate([values, spare], 1)
    return jnp.take_along_axis(wide, column, axis=1, mode="promise_in_bounds")


def sample_kernel(half, orders, cycles, lists, block, phi, psi, frac, phase, *index):
    scale = 2.0 / math.sqrt(phase.shape[2] * MPRIME)
    band = lax.axis_index("band")
    eight = phase.shape[2]
    row = lax.broadcasted_iota(jnp.int32, (eight, LANES), 0)
    orders = jnp.broadcast_to(orders[...], (eight, orders.shape[1]))
    order = own_lanes(orders, band ^ (half * (eight // 2) + row // 2))
    step = order.astype(jnp.float32) * (1.0 / NPHI)
    quarter = (row & 1).astype(jnp.float32) * 0.25
    sources, entries = lists.shape[:2]
    codes = jnp.concatenate([lists[source] for source in range(sources)], 0)
    codes = jnp.maximum(own_lanes(codes, jnp.full((codes.shape[0], LANES), band)), 0)
    for h in range(0, block.shape[0], eight):
        blocks = block[h : h + eight, :]
        start = jnp.zeros_like(blocks)
        cycle = jnp.zeros_like(blocks)
        for entry in range(sources * entries):
            code = codes[entry : entry + 1, :]
            here = blocks == entry
            start = jnp.where(here, code & (NPHI - 1), start)
            if index:
                source = entry // entries
                for slot in range(cycles.shape[0]):
                    kept = here & (code >= slot * NPHI)
                    cycle = jnp.where(kept, cycles[slot : slot + 1, source : source + 1], cycle)
        if index:
            index[0][h : h + eight, :] = cycle * NPSI + psi[h : h + eight, :]
        first = ((start + phi[h : h + eight, :]) & (NPHI - 1)).astype(jnp.float32)
        for g in range(eight):
            f = frac[0, h + g : h + g + 1, :]
            here = step * first[g : g + 1, :] + quarter
            at = cosine(here).astype(jnp.bfloat16).astype(jnp.float32)
            after = cosine(here + step).astype(jnp.bfloat16).astype(jnp.float32)
            weight = (at + f * (after - at)) * scale
            phase[0, h + g] = weight
            phase[1, h + g] = weight * frac[1, h + g : h + g + 1, :]


def pick_lanes(values, column):
    inside = column & (LANES - 1)
    picked = None
    for first in range(0, values.shape[1], LANES):
        tile = values[:, first : first + LANES]
        spare = LANES - tile.shape[1]
        if spare:
            tile = jnp.concatenate([tile, jnp.zeros((tile.shape[0], spare), tile.dtype)], 1)
        found = jnp.take_along_axis(tile, inside, axis=1, mode="promise_in_bounds")
        picked = found if picked is None else jnp.where(column >= first, found, picked)
    return picked


def psi_weights(width):
    shape = (2 * ROWS, width)
    lane = lax.broadcasted_iota(jnp.int32, shape, 1) & (NPSI - 1)
    line = lax.broadcasted_iota(jnp.int32, shape, 0)
    imag = line >= ROWS
    n = jnp.where(imag, line - ROWS, line)
    turns = ((n - BMAX) * lane).astype(jnp.float32) * (1.0 / NPSI)
    c, s = cosine(turns), cosine(turns - 0.25)
    return jnp.where(imag, -s, c), jnp.where(imag, c, s)


def multipole_sum(part, beams, sky, w):
    chunk = w.shape[1]
    lanes = slice(part * chunk, (part + 1) * chunk)
    pieces = []
    for beam in beams:
        real = imag = 0.0
        for c in range(sky.shape[0]):
            sr, si = sky[c, 0], sky[c, 1]
            br, bi = beam[c, 0, :, lanes], beam[c, 1, :, lanes]
            real += sr * br + si * bi
            imag += si * br - sr * bi
        pieces += [real, imag]
    mixed = jnp.concatenate(pieces, 0).astype(jnp.bfloat16)
    return lax.dot_general(
        mixed, w[...], (((1,), (1,)), ((), ())), preferred_element_type=jnp.float32
    )


def near_kernel(beam_own, beam_other, sky, w, total, weights):
    total[...] = multipole_sum(0, (beam_own, beam_other), sky, w)
    weights[0], weights[1] = psi_weights(weights.shape[2])


def rows_kernel(beam_own, beam_other, sky, w, near, weights, out):
    cycles = w.shape[0] // MPRIME
    total = near[...] + multipole_sum(1, (beam_own, beam_other), sky, w)
    shape = (total.shape[0], weights.shape[2])
    order = lax.rem(lax.broadcasted_iota(jnp.int32, shape, 0), ROWS)
    cycle = lax.div(lax.broadcasted_iota(jnp.int32, shape, 1), NPSI)
    column = jnp.minimum(order, MPRIME - 1) * cycles + cycle
    coeff = jnp.concatenate(
        [pick_lanes(total, column[:, t : t + LANES]) for t in range(0, shape[1], LANES)], 1
    )
    for side in range(2):
        held = coeff[side * 2 * ROWS : (side + 1) * 2 * ROWS]
        for s in range(2):
            out[side, s : s + 1, :] = jnp.sum(held * weights[s], 0, keepdims=True)


def to_next_psi(part):
    width = part.shape[1]
    last = lax.broadcasted_iota(jnp.int32, part.shape, 1) & (NPSI - 1) == NPSI - 1
    after = jnp.where(last, pltpu.roll(part, NPSI - 1, 1), pltpu.roll(part, width - 1, 1))
    return after - part


def half_sum(part, change, phase, low, g):
    at = jnp.broadcast_to(low[g : g + 1, :], (part.shape[0], LANES))
    return pick_lanes(part, at) * phase[0, g] + pick_lanes(change, at) * phase[1, g]


def first_half_kernel(held, received, phase, low, out):
    parts = (held[0, 0], held[1, 1], received[0, 1], received[1, 0])
    part = jnp.concatenate([rows.astype(jnp.float32) for rows in parts], 0)
    change = to_next_psi(part)
    for g in range(out.shape[0]):
        out[g] = half_sum(part, change, phase, low, g)


def row_sums(tiles):
    row = lax.broadcasted_iota(jnp.int32, tiles[0].shape, 0)
    for step in (1, 2, 4):
        upper = (row & step) != 0
        tiles = [
            jnp.where(upper, b, a) + pltpu.roll(jnp.where(upper, a, b), step, 0)
            for a, b in zip(tiles[::2], tiles[1::2])
        ]
    return tiles[0]


def second_half_kernel(received, first, phase, low, out):
    part = jnp.concatenate([received[k].astype(jnp.float32) for k in range(received.shape[0])], 0)
    change = to_next_psi(part)
    for g in range(0, out.shape[0], 8):
        totals = [
            first[k] + half_sum(part, change, phase, low, k) for k in range(g, g + 8)
        ]
        out[g : g + 8, :] = row_sums(totals)


def call(kernel, out_shape, in_specs):
    return pl.pallas_call(
        kernel,
        out_shape=out_shape,
        in_specs=in_specs,
        out_specs=jax.tree.map(lambda _: vmem(), out_shape),
        cost_estimate=pl.CostEstimate(flops=1, bytes_accessed=1, transcendentals=0),
        compiler_params=pltpu.CompilerParams(vmem_limit_bytes=24 << 20),
    )


def by_samples(
    sky_coeffs,
    beam_coeffs,
    wigner_panel,
    m_values,
    cycle_table,
    send_lists,
    sample_block,
    sample_phi,
    sample_psi,
    sample_frac,
):
    f32 = jnp.float32
    bands = lax.axis_size("band")
    chunk, cycles = wigner_panel.shape[2:]
    groups = sample_block.shape[1] // LANES
    psi_width = cycles * NPSI

    sizes = (bands, lax.axis_size("det"))

    def swap(x, band_bits, det_bits):
        pairs = [
            (b * sizes[1] + d, (b ^ band_bits) * sizes[1] + (d ^ det_bits))
            for b in range(sizes[0])
            for d in range(sizes[1])
        ]
        return lax.ppermute(x, ("band", "det"), pairs)

    panel = jnp.transpose(wigner_panel[0], (0, 2, 1)).reshape(MPRIME * cycles, chunk)
    panel_other = swap(panel, 0, 3)
    sky_other = swap(sky_coeffs, 0, 3)
    beam = jnp.transpose(beam_coeffs[0], (0, 2, 1, 3))
    beam_other = swap(beam, 0, 1)
    split = jax.ShapeDtypeStruct((beam.shape[0], 2, ROWS, 2 * chunk), f32)
    beam_own = call(beam_kernel, split, [vmem()])(beam)
    beam_other = call(beam_kernel, split, [vmem()])(beam_other)
    near_sum, psi = call(
        near_kernel,
        (
            jax.ShapeDtypeStruct((4 * ROWS, MPRIME * cycles), f32),
            jax.ShapeDtypeStruct((2, 2 * ROWS, psi_width), f32),
        ),
        [vmem()] * 4,
    )(beam_own, beam_other, sky_coeffs, panel)
    sums = call(rows_kernel, jax.ShapeDtypeStruct((2, 2, psi_width), f32), [vmem()] * 6)(
        beam_own, beam_other, sky_other, panel_other, near_sum, psi
    )
    rows = (sums + swap(sums, 0, 1)[::-1]).astype(jnp.bfloat16)
    rows_y = swap(rows, 1, 1)
    weights = jax.ShapeDtypeStruct((groups, bands, LANES), f32)
    index = jax.ShapeDtypeStruct((groups, LANES), jnp.int32)
    two = jax.ShapeDtypeStruct((2, *weights.shape), f32)
    frac = sample_frac.reshape(2, groups, LANES)
    where = (sample_block, sample_phi, sample_psi)
    lists = (m_values.reshape(1, -1), cycle_table.T, jnp.transpose(send_lists[0], (0, 2, 1)))
    samples = (*lists, *(a.reshape(groups, LANES) for a in where), frac)
    late, _ = lax.optimization_barrier((samples[0], rows))
    near, low = call(
        functools.partial(sample_kernel, 0), (two, index), [vmem()] * 7
    )(late, *samples[1:])
    rows_y, near = lax.optimization_barrier((rows_y, near))
    pair = jnp.stack([rows, rows_y])
    pair_z = swap(pair, 2, 1)
    late, _ = lax.optimization_barrier((samples[0], pair))
    far = call(functools.partial(sample_kernel, 1), two, [vmem()] * 7)(late, *samples[1:])
    pair_z, far = lax.optimization_barrier((pair_z, far))
    rest = swap(jnp.stack([pair[0, 1], pair[1, 0], pair_z[0, 0], pair_z[1, 1]]), 4, 1)
    first = call(first_half_kernel, weights, [vmem()] * 4)(pair, pair_z, near, low)
    values = call(
        second_half_kernel, jax.ShapeDtypeStruct((groups, LANES), f32), [vmem()] * 4
    )(rest, first, far, low)
    return values.reshape(1, -1)


def solution(mesh):
    def per_device(*args):
        cycles = args[2].shape[3]
        small = mesh.shape["band"] == 8 and cycles <= 8
        return (by_samples if small else by_blocks)(*args)

    return jax.shard_map(
        per_device,
        mesh=mesh,
        in_specs=(
            P(None, None, "band", "det"),
            P("det", None, None, None, None),
            P("band", None, "det", None),
            P(),
            P(),
            P("det", None, None, None),
            P("det", "band"),
            P("det", "band"),
            P("det", "band"),
            P(None, "det", "band"),
        ),
        out_specs=P("det", "band"),
        check_vma=False,
    )
```
